512 devices in a mesh: dp: 8 (over x, y_hi), ctx: 64 (over y_lo, z, core).
Axes of the slice: x: 4, y: 8 (y_hi: 2, y_lo: 4; y = y_hi * 4 + y_lo), z: 8, core: 2. Of those that a mesh axis runs over, the one named last changes fastest.
Arguments:
- gated_input: bfloat16 [8, 49152, 1024], P('dp', 'ctx'), may hold values from -6 to 6
- upstream: bfloat16 [8, 49152, 1024], P('dp', 'ctx'), may hold values from -6 to 6
- depth_kernel: float32 [31, 1024], replicated, may hold values from -1 to 1
- carried_error: float32 [8, 1024, 1024], P('dp', 'ctx'), may hold values from -6 to 6
- right_init: float32 [1024, 64], replicated, may hold values from -6 to 6
Outputs:
- right_factor: float32 [1024, 64], replicated
- estimate: float32 [1024, 1024], P('ctx')
- updated_error: float32 [8, 1024, 1024], P('dp', 'ctx')
The draws below stay inside these ranges and needn't reach their ends.
All inputs are finite; a program needn't handle non-finite values.
Results may differ from the reference program's by a relative error of at most 0.0019.
Values may be sent and summed in bfloat16 or wider, within the bound.
No kernel may reach another device: no remote copies, remote signals or barrier semaphores. Data moves between devices by JAX's collectives and lax.ppermute only.
A program may use at most 64 MiB of HBM per device.

```python
import math
from functools import partial
import jax
import jax.numpy as jnp
from jax import lax

CH = 1024
OUT = 1024
RANK = 64
KERNEL = 31
FRAMES = 49152
N_DP = 8


def block_levels(key, shape, split, least, largest):
    factor_of = 1.0
    for dim, parts in split:
        heights = jax.random.uniform(jax.random.fold_in(jax.random.fold_in(key, 6), dim), (parts,), jnp.float32, least / len(split), largest / len(split))
        factor_of = factor_of * jnp.repeat(jnp.exp(heights), shape[dim] // parts).reshape((-1,) + (1,) * (len(shape) - 1 - dim))
    return factor_of


def normal_values(stream_key, shape, scale, bound, cuts=(), held_as=jnp.bfloat16):
    factor_of = block_levels(stream_key, shape, cuts, -0.22, 0.18) if cuts else 1.0
    values = jax.random.normal(stream_key, shape, jnp.float32) * scale * factor_of
    return jnp.minimum(jnp.maximum(values, -bound), bound).astype(held_as)


def setup_inputs(seed: int = 0) -> dict:
    splits = jax.random.split(jax.random.key(seed), 6)
    return {
        "gated_input": normal_values(splits[0], (N_DP, FRAMES, CH), 1.0, 6.0, ((0, 8), (1, 64))),
        "upstream": normal_values(splits[1], (N_DP, FRAMES, OUT), 1.0, 6.0, ((0, 8), (1, 64))),
        "depth_kernel": normal_values(splits[2], (KERNEL, CH), KERNEL ** -0.5, 1.0, (), jnp.float32),
        "carried_error": normal_values(splits[3], (N_DP, CH, OUT), 1.0, 6.0, ((0, 8), (1, 64)), jnp.float32),
        "right_init": normal_values(splits[4], (OUT, RANK), 1.0, 6.0, (), jnp.float32),
    }


def replica_gradient(depth_kernel, pair):
    gated, signal = pair
    rim_width = (KERNEL - 1) // 2
    padded = jnp.pad(gated.astype(jnp.float32), ((rim_width, rim_width), (0, 0)))
    summed = jnp.zeros((FRAMES, CH), jnp.float32)
    for tap_index in range(KERNEL):
        summed = summed + depth_kernel[tap_index] * padded[tap_index:tap_index + FRAMES]
    activation = (summed * jax.nn.sigmoid(summed)).astype(jnp.bfloat16)
    return lax.dot_general(activation.astype(jnp.float32), signal.astype(jnp.float32), (((0,), (0,)), ((), ())), preferred_element_type=jnp.float32)

def reference(gated_input, upstream, depth_kernel, carried_error, right_init):
    inverse_root = 1.0 / math.sqrt(FRAMES)
    gradients = lax.map(partial(replica_gradient, depth_kernel), (gated_input, upstream))
    merged = gradients * inverse_root + carried_error
    left = jnp.einsum('dco,or->cr', merged, right_init, precision=lax.Precision.HIGHEST)
    gram_matrix = jnp.dot(left.T, left, precision=lax.Precision.HIGHEST)
    factor = jnp.linalg.cholesky(gram_matrix)
    left_hat = lax.linalg.triangular_solve(factor, left, left_side=False, lower=True, transpose_a=True)
    right_factor = jnp.einsum('dco,cr->or', merged, left_hat, precision=lax.Precision.HIGHEST) / N_DP
    estimate = jnp.dot(left_hat, right_factor.T, precision=lax.Precision.HIGHEST)
    updated_error = merged - estimate[None]
    return (right_factor, estimate, updated_error)
```

```python
import functools
import math

import jax
import jax.numpy as jnp
from jax import lax
from jax.experimental import pallas as pl
from jax.experimental.pallas import tpu as pltpu
from jax.sharding import Mesh, PartitionSpec as P

F32 = jnp.float32
BF16 = jnp.bfloat16
HIGHEST = lax.Precision.HIGHEST
DP = ("x", "h")
CTX = ("y", "z", "c")
CHIPS = ("y", "z")
NEAR = ("x", "z")
FAR = ("h", "y", "c")
RIM = 16
BLOCK = 256
STEP = 96
PARAMS = pltpu.CompilerParams(vmem_limit_bytes=48 << 20)


def conv_kernel(core_ref, x_ref, low_ref, high_ref, taps_ref, up_ref, keep_ref, send_ref, wide_ref, act_ref):
    frames, width = x_ref.shape
    wide_ref[0:RIM] = low_ref[...].astype(F32)
    wide_ref[RIM : RIM + frames] = x_ref[...].astype(F32)
    wide_ref[RIM + frames :] = high_ref[...].astype(F32)
    for lane in range(0, width, 128):
        cols = slice(lane, lane + 128)

        def chunk(index, _):
            base = pl.multiple_of(index * STEP, STEP)
            rows = wide_ref[pl.ds(base, STEP + 2 * RIM), cols]
            total = None
            for shift in range(8):
                part = None
                for tile in range(4):
                    tap = 8 * tile + shift
                    if tap == 0:
                        continue
                    term = taps_ref[tap : tap + 1, cols] * rows[8 * tile : 8 * tile + STEP + 8]
                    part = term if part is None else part + term
                if shift:
                    part = pltpu.roll(part, STEP + 8 - shift, 0)
                part = part[:STEP]
                total = part if total is None else total + part
            half = 0.5 * total
            act_ref[pl.ds(base, STEP), cols] = (half + half * jnp.tanh(half)).astype(BF16)
            return 0

        lax.fori_loop(0, frames // STEP, chunk, 0)
    product = lax.dot_general(
        act_ref[...], up_ref[...], (((0,), (0,)), ((), ())), preferred_element_type=F32
    )
    pieces = product.reshape(width // 32, 2, 16, product.shape[1])
    first = pieces[:, 0].reshape(width // 2, -1)
    second = pieces[:, 1].reshape(width // 2, -1)

    @pl.when(core_ref[0] == 0)
    def _():
        keep_ref[...] = first
        send_ref[...] = second

    @pl.when(core_ref[0] == 1)
    def _():
        keep_ref[...] = second
        send_ref[...] = first


def conv_product(core, block, low, high, taps, signal):
    frames, channels = block.shape
    features = signal.shape[1]
    half = jax.ShapeDtypeStruct((channels // 2, features), F32)
    column = lambda rows: pl.BlockSpec((rows, BLOCK), lambda i: (0, i))
    return pl.pallas_call(
        conv_kernel,
        grid=(channels // BLOCK,),
        in_specs=[
            pl.BlockSpec(memory_space=pltpu.SMEM),
            column(frames),
            column(RIM),
            column(RIM),
            column(taps.shape[0]),
            pl.BlockSpec((frames, features), lambda i: (0, 0)),
        ],
        out_specs=[pl.BlockSpec((BLOCK // 2, features), lambda i: (i, 0))] * 2,
        out_shape=[half, half],
        scratch_shapes=[pltpu.VMEM((frames + 2 * RIM, BLOCK), F32), pltpu.VMEM((frames, BLOCK), BF16)],
        compiler_params=PARAMS,
        name="conv_product",
    )(core, block, low, high, taps, signal)


def merge_kernel(inverse_root, parts_ref, carried_ref, right_ref, merged_ref, left_ref):
    total = parts_ref[0].astype(F32)
    for index in range(1, parts_ref.shape[0]):
        total = total + parts_ref[index].astype(F32)
    merged = total * inverse_root + carried_ref[...]
    merged_ref[...] = merged
    left = lax.dot_general(
        merged, right_ref[...], (((1,), (1,)), ((), ())), precision=HIGHEST, preferred_element_type=F32
    )
    for index in range(left_ref.shape[0]):
        left_ref[index] = left


def term_kernel(parts_ref, merged_ref, left_ref, term_ref):
    left = parts_ref[0]
    for index in range(1, parts_ref.shape[0]):
        left = left + parts_ref[index]
    left_ref[...] = left
    share = left * (1.0 / parts_ref.shape[0])
    joined = jnp.concatenate([merged_ref[...], jnp.zeros_like(left), share], axis=1)
    term = lax.dot_general(
        left, joined, (((0,), (0,)), ((), ())), precision=HIGHEST, preferred_element_type=F32
    )
    for index in range(term_ref.shape[0]):
        term_ref[index] = term[2 * index : 2 * index + 2]


def total_kernel(parts_ref, total_ref):
    total = parts_ref[0]
    for index in range(1, parts_ref.shape[0]):
        total = total + parts_ref[index]
    for index in range(total_ref.shape[0]):
        total_ref[index] = total


def finish_kernel(replicas, rows_ref, left_ref, merged_ref, right_ref, estimate_ref, error_ref, wide_ref):
    rank = left_ref.shape[1]
    features = merged_ref.shape[1]
    for index in range(rows_ref.shape[0]):
        wide_ref[2 * index : 2 * index + 2] = rows_ref[index]
    row = lax.broadcasted_iota(jnp.int32, (rank, 2 * rank), 0)
    lane = lax.broadcasted_iota(jnp.int32, (rank, 2 * rank), 1)
    work = wide_ref[:, features:] + (row == lane).astype(F32)
    for step in range(rank - 1):
        column = work[:, rank + step : rank + step + 1]
        pivot_row = work[step : step + 1]
        scaled = pivot_row / pivot_row[:, rank + step : rank + step + 1]
        work = work - jnp.where(row > step, column, 0.0) * scaled
    pivots = jnp.sum(jnp.where(row + rank == lane, work, 0.0), axis=1, keepdims=True)
    inverse = (work * (1.0 / jnp.sqrt(pivots)))[:, :rank]
    dot = functools.partial(lax.dot_general, precision=HIGHEST, preferred_element_type=F32)
    right = dot(inverse, wide_ref[:, :features], (((1,), (0,)), ((), ()))) * (1.0 / replicas)
    right_ref[...] = right
    left_hat = dot(left_ref[...], inverse, (((1,), (1,)), ((), ())))
    estimate = dot(left_hat, right, (((1,), (0,)), ((), ())))
    estimate_ref[...] = estimate
    error_ref[...] = merged_ref[...] - estimate


def call(kernel, outs, *args, scratch=()):
    return pl.pallas_call(
        kernel,
        out_shape=[jax.ShapeDtypeStruct(shape, F32) for shape in outs],
        scratch_shapes=list(scratch),
        compiler_params=PARAMS,
        name=getattr(kernel, "func", kernel).__name__,
    )(*args)


def exchange(block, axes):
    return lax.all_to_all(block, axes, 0, 0, tiled=True)


def local(gated_input, upstream, depth_kernel, carried_error, right_init):
    replicas = lax.axis_size(DP)
    contexts = lax.axis_size(CTX)
    chips = lax.axis_size(CHIPS)
    near, far = lax.axis_size(NEAR), lax.axis_size(FAR)
    block = gated_input[0]
    frames, channels = block.shape
    features = upstream.shape[2]
    rank = right_init.shape[1]
    owned = channels // contexts
    forward = [(i, i + 1) for i in range(contexts - 1)]
    backward = [(target, source) for source, target in forward]
    low = lax.ppermute(block[frames - RIM :], CTX, forward)
    high = lax.ppermute(block[:RIM], CTX, backward)
    taps = jnp.pad(depth_kernel, ((1, 0), (0, 0)))
    core = lax.axis_index("c").reshape(1)
    keep, send = conv_product(core, block, low, high, taps, upstream[0])
    received = lax.ppermute(send, "c", [(0, 1), (1, 0)])
    pair_sum = (keep + received).astype(BF16)
    parts = exchange(pair_sum, CHIPS).reshape(chips, owned, features)
    inverse_root = 1.0 / math.sqrt(frames * contexts)
    merged, left_parts = call(
        functools.partial(merge_kernel, inverse_root),
        [(owned, features), (replicas, owned, rank)],
        parts,
        carried_error[0],
        right_init.T,
    )
    left_parts = exchange(left_parts, DP)
    width = features + 2 * rank
    pair = rank // near
    left, term = call(term_kernel, [(owned, rank), (near, pair, width)], left_parts, merged)
    (near_sum,) = call(total_kernel, [(far, pair, width)], exchange(term, NEAR))
    (far_sum,) = call(total_kernel, [(near, pair, width)], exchange(near_sum, FAR))
    right, estimate, error = call(
        functools.partial(finish_kernel, replicas),
        [(rank, features), (owned, features), (owned, features)],
        exchange(far_sum, NEAR),
        left,
        merged,
        scratch=[pltpu.VMEM((rank, width), F32)],
    )
    return right.T, estimate, error[None]


def solution(mesh):
    wide = Mesh(mesh.devices.reshape(4, 2, 4, 8, 2), ("x", "h", "y", "z", "c"))
    return jax.shard_map(
        local,
        mesh=wide,
        in_specs=(P(DP, CTX, None), P(DP, CTX, None), P(), P(DP, CTX, None), P()),
        out_specs=(P(), P(CTX, None), P(DP, CTX, None)),
        check_vma=False,
    )
```

```python
import functools
import math

import jax
import jax.numpy as jnp
from jax import lax
from jax.experimental import pallas as pl
from jax.experimental.pallas import tpu as pltpu
from jax.sharding import Mesh, PartitionSpec as P

F32 = jnp.float32
BF16 = jnp.bfloat16
HIGHEST = lax.Precision.HIGHEST
DP = ("x", "h")
CTX = ("y", "z", "c")
CHIPS = ("y", "z")
RIM = 16
BLOCK = 256
STEP = 96
PANEL = 8
PARAMS = pltpu.CompilerParams(vmem_limit_bytes=48 << 20)


def conv_kernel(core_ref, x_ref, low_ref, high_ref, taps_ref, up_ref, keep_ref, send_ref, wide_ref, act_ref):
    frames, width = x_ref.shape
    wide_ref[0:RIM] = low_ref[...].astype(F32)
    wide_ref[RIM : RIM + frames] = x_ref[...].astype(F32)
    wide_ref[RIM + frames :] = high_ref[...].astype(F32)
    for lane in range(0, width, 128):
        cols = slice(lane, lane + 128)

        def chunk(index, _):
            base = pl.multiple_of(index * STEP, STEP)
            rows = wide_ref[pl.ds(base, STEP + 2 * RIM), cols]
            total = None
            for shift in range(8):
                part = None
                for tile in range(4):
                    tap = 8 * tile + shift
                    if tap == 0:
                        continue
                    term = taps_ref[tap - 1 : tap, cols] * rows[8 * tile : 8 * tile + STEP + 8]
                    part = term if part is None else part + term
                if shift:
                    part = pltpu.roll(part, STEP + 8 - shift, 0)
                part = part[:STEP]
                total = part if total is None else total + part
            half = 0.5 * total
            act_ref[pl.ds(base, STEP), cols] = (half + half * jnp.tanh(half)).astype(BF16)
            return 0

        lax.fori_loop(0, frames // STEP, chunk, 0)
    product = lax.dot_general(
        act_ref[...], up_ref[...], (((0,), (0,)), ((), ())), preferred_element_type=F32
    )
    pieces = product.reshape(width // 32, 2, 16, product.shape[1])
    first = pieces[:, 0].reshape(width // 2, -1)
    second = pieces[:, 1].reshape(width // 2, -1)

    @pl.when(core_ref[0] == 0)
    def _():
        keep_ref[...] = first
        send_ref[...] = second

    @pl.when(core_ref[0] == 1)
    def _():
        keep_ref[...] = second
        send_ref[...] = first


def conv_product(core, block, low, high, taps, signal):
    frames, channels = block.shape
    features = signal.shape[1]
    half = jax.ShapeDtypeStruct((channels // 2, features), F32)
    column = lambda rows: pl.BlockSpec((rows, BLOCK), lambda i: (0, i))
    return pl.pallas_call(
        conv_kernel,
        grid=(channels // BLOCK,),
        in_specs=[
            pl.BlockSpec(memory_space=pltpu.SMEM),
            column(frames),
            column(RIM),
            column(RIM),
            column(taps.shape[0]),
            pl.BlockSpec((frames, features), lambda i: (0, 0)),
        ],
        out_specs=[pl.BlockSpec((BLOCK // 2, features), lambda i: (i, 0))] * 2,
        out_shape=[half, half],
        scratch_shapes=[pltpu.VMEM((frames + 2 * RIM, BLOCK), F32), pltpu.VMEM((frames, BLOCK), BF16)],
        compiler_params=PARAMS,
        name="conv_product",
    )(core, block, low, high, taps, signal)


def merge_kernel(inverse_root, parts_ref, carried_ref, merged_ref, copies_ref):
    total = parts_ref[0].astype(F32)
    for index in range(1, parts_ref.shape[0]):
        total = total + parts_ref[index].astype(F32)
    merged = total * inverse_root + carried_ref[...]
    merged_ref[...] = merged
    for index in range(copies_ref.shape[0]):
        copies_ref[index] = merged


def term_kernel(parts_ref, right_ref, left_ref, term_ref):
    mean = parts_ref[0]
    for index in range(1, parts_ref.shape[0]):
        mean = mean + parts_ref[index]
    left = lax.dot_general(
        mean, right_ref[...], (((1,), (1,)), ((), ())), precision=HIGHEST, preferred_element_type=F32
    )
    left_ref[...] = left
    joined = jnp.concatenate([mean, jnp.zeros_like(left), left], axis=1)
    term = lax.dot_general(
        left, joined, (((0,), (0,)), ((), ())), precision=HIGHEST, preferred_element_type=F32
    )
    for index in range(term_ref.shape[0]):
        term_ref[index] = term[index : index + 1]


def total_kernel(parts_ref, total_ref):
    total = parts_ref[0]
    for index in range(1, parts_ref.shape[0]):
        total = total + parts_ref[index]
    for index in range(total_ref.shape[0]):
        total_ref[index] = total


def eliminate(rest, rank):
    done = []
    for start in range(0, rank, PANEL):
        row = lax.broadcasted_iota(jnp.int32, rest.shape, 0)
        first = rank + start
        columns = [
            jnp.broadcast_to(rest[:, first + j : first + j + 1], rest.shape) for j in range(PANEL)
        ]
        top = rest[:PANEL]
        scaled = []
        for j in range(PANEL):
            inverse = 1.0 / columns[j][j : j + 1]
            scaled.append(top[j : j + 1] * inverse)
            below = jnp.where(row > j, columns[j], 0.0)
            columns[j] = below
            for i in range(j + 1, PANEL):
                columns[i] = columns[i] - below * (columns[i][j : j + 1] * inverse)
            top = top - below[:PANEL] * scaled[j]
        done.append(top)
        rest = rest[PANEL:]
        if start + PANEL < rank:
            for j in range(PANEL):
                rest = rest - columns[j][PANEL:] * scaled[j]
    return jnp.concatenate(done, axis=0)


def finish_kernel(replicas, rows_ref, left_ref, merged_ref, right_ref, estimate_ref, error_ref, wide_ref):
    rank = left_ref.shape[1]
    features = merged_ref.shape[1]
    for index in range(rows_ref.shape[0]):
        wide_ref[index : index + 1] = rows_ref[index]
    row = lax.broadcasted_iota(jnp.int32, (rank, 2 * rank), 0)
    lane = lax.broadcasted_iota(jnp.int32, (rank, 2 * rank), 1)
    work = eliminate(wide_ref[:, features:] + (row == lane).astype(F32), rank)
    pivots = jnp.sum(jnp.where(row + rank == lane, work, 0.0), axis=1, keepdims=True)
    inverse = (work * (1.0 / jnp.sqrt(pivots)))[:, :rank]
    dot = functools.partial(lax.dot_general, precision=HIGHEST, preferred_element_type=F32)
    right = dot(inverse, wide_ref[:, :features], (((1,), (0,)), ((), ()))) * (1.0 / replicas)
    right_ref[...] = right
    left_hat = dot(left_ref[...], inverse, (((1,), (1,)), ((), ())))
    estimate = dot(left_hat, right, (((1,), (0,)), ((), ())))
    estimate_ref[...] = estimate
    error_ref[...] = merged_ref[...] - estimate


def call(kernel, outs, *args, scratch=()):
    return pl.pallas_call(
        kernel,
        out_shape=[jax.ShapeDtypeStruct(shape, F32) for shape in outs],
        scratch_shapes=list(scratch),
        compiler_params=PARAMS,
        name=getattr(kernel, "func", kernel).__name__,
    )(*args)


def exchange(block, axes):
    return lax.all_to_all(block, axes, 0, 0, tiled=True)


def local(gated_input, upstream, depth_kernel, carried_error, right_init):
    replicas = lax.axis_size(DP)
    contexts = lax.axis_size(CTX)
    chips = lax.axis_size(CHIPS)
    block = gated_input[0]
    frames, channels = block.shape
    features = upstream.shape[2]
    rank = right_init.shape[1]
    owned = channels // contexts
    forward = [(i, i + 1) for i in range(contexts - 1)]
    backward = [(target, source) for source, target in forward]
    low = lax.ppermute(block[frames - RIM :], CTX, forward)
    high = lax.ppermute(block[:RIM], CTX, backward)
    core = lax.axis_index("c").reshape(1)
    keep, send = conv_product(core, block, low, high, depth_kernel, upstream[0])
    received = lax.ppermute(send, "c", [(0, 1), (1, 0)])
    pair_sum = (keep + received).astype(BF16)
    parts = exchange(pair_sum, CHIPS).reshape(chips, owned, features)
    inverse_root = 1.0 / math.sqrt(frames * contexts)
    merged, copies = call(
        functools.partial(merge_kernel, inverse_root),
        [(owned, features), (replicas, owned, features)],
        parts,
        carried_error[0],
    )
    width = features + 2 * rank
    left, term = call(
        term_kernel, [(owned, rank), (rank, 1, width)], exchange(copies, DP), right_init.T
    )
    (total,) = call(total_kernel, [(rank, 1, width)], exchange(term, CTX))
    right, estimate, error = call(
        functools.partial(finish_kernel, replicas),
        [(rank, features), (owned, features), (owned, features)],
        exchange(total, CTX),
        left,
        merged,
        scratch=[pltpu.VMEM((rank, width), F32)],
    )
    return right.T, estimate, error[None]


def solution(mesh):
    wide = Mesh(mesh.devices.reshape(4, 2, 4, 8, 2), ("x", "h", "y", "z", "c"))
    return jax.shard_map(
        local,
        mesh=wide,
        in_specs=(P(DP, CTX, None), P(DP, CTX, None), P(), P(DP, CTX, None), P()),
        out_specs=(P(), P(CTX, None), P(DP, CTX, None)),
        check_vma=False,
    )
```

```python
import functools
import math

import jax
import jax.numpy as jnp
from jax import lax
from jax.experimental import pallas as pl
from jax.experimental.pallas import tpu as pltpu
from jax.sharding import Mesh, PartitionSpec as P

F32 = jnp.float32
BF16 = jnp.bfloat16
HIGHEST = lax.Precision.HIGHEST
DP = ("x", "h")
CTX = ("y", "z", "c")
ROWS = ("x", "h", "y")
NEAR = ("x", "z")
FAR = ("h", "y", "c")
RIM = 16
BLOCK = 256
STEP = 192
PANEL = 8
PARAMS = pltpu.CompilerParams(vmem_limit_bytes=48 << 20)


def conv_kernel(
    core_ref, block_hbm, low_ref, high_ref, taps_hbm, up_hbm, keep_ref, send_ref,
    block_ref, taps_ref, up_ref, wide_ref, act_ref, sems,
):
    frames, width = act_ref.shape
    count = block_ref.shape[0]
    step = pl.program_id(0)

    def block_copy(index):
        cols = pl.ds(pl.multiple_of(index * width, width), width)
        return pltpu.make_async_copy(block_hbm.at[:, cols], block_ref.at[index], sems.at[index])

    taps_copy = pltpu.make_async_copy(taps_hbm, taps_ref, sems.at[count])
    up_copy = pltpu.make_async_copy(up_hbm, up_ref, sems.at[count + 1])

    @pl.when(step == 0)
    def _():
        block_copy(0).start()
        taps_copy.start()
        for index in range(1, count):
            block_copy(index).start()
        up_copy.start()
        taps_copy.wait()

    block_copy(step).wait()
    wide_ref[0:RIM] = low_ref[...].astype(F32)
    wide_ref[RIM : RIM + frames] = block_ref[step].astype(F32)
    wide_ref[RIM + frames :] = high_ref[...].astype(F32)
    for lane in range(0, width, 128):
        cols = slice(lane, lane + 128)
        tap_cols = pl.ds(pl.multiple_of(step * width + lane, 128), 128)

        def chunk(index, _):
            base = pl.multiple_of(index * STEP, STEP)
            rows = wide_ref[pl.ds(base, STEP + 2 * RIM), cols]
            total = None
            for shift in range(8):
                part = None
                for tile in range(4):
                    tap = 8 * tile + shift
                    if tap == 0:
                        continue
                    term = taps_ref[tap - 1 : tap, tap_cols] * rows[8 * tile : 8 * tile + STEP + 8]
                    part = term if part is None else part + term
                if shift:
                    part = pltpu.roll(part, STEP + 8 - shift, 0)
                part = part[:STEP]
                total = part if total is None else total + part
            half = 0.5 * total
            act_ref[pl.ds(base, STEP), cols] = (half + half * jnp.tanh(half)).astype(BF16)
            return 0

        lax.fori_loop(0, frames // STEP, chunk, 0)

    @pl.when(step == 0)
    def _():
        up_copy.wait()

    product = lax.dot_general(
        act_ref[...], up_ref[...], (((0,), (0,)), ((), ())), preferred_element_type=F32
    )
    pieces = product.reshape(width // 32, 2, 16, product.shape[1])
    first, second = pieces[:, 0][:, None], pieces[:, 1][:, None]

    @pl.when(core_ref[0] == 0)
    def _():
        keep_ref[...] = first
        send_ref[...] = second

    @pl.when(core_ref[0] == 1)
    def _():
        keep_ref[...] = second
        send_ref[...] = first


def conv_product(core, block, low, high, taps, signal):
    frames, channels = block.shape
    features = signal.shape[1]
    count = channels // BLOCK
    half = jax.ShapeDtypeStruct((BLOCK // 32, count, 16, features), F32)
    rim = pl.BlockSpec((RIM, BLOCK), lambda i: (0, i))
    far = pl.BlockSpec(memory_space=pltpu.HBM)
    block, taps, signal = (
        pltpu.with_memory_space_constraint(array, pltpu.HBM) for array in (block, taps, signal)
    )
    return pl.pallas_call(
        conv_kernel,
        grid=(count,),
        in_specs=[pl.BlockSpec(memory_space=pltpu.SMEM), far, rim, rim, far, far],
        out_specs=[pl.BlockSpec((BLOCK // 32, 1, 16, features), lambda i: (0, i, 0, 0))] * 2,
        out_shape=[half, half],
        scratch_shapes=[
            pltpu.VMEM((count, frames, BLOCK), BF16),
            pltpu.VMEM(taps.shape, F32),
            pltpu.VMEM(signal.shape, BF16),
            pltpu.VMEM((frames + 2 * RIM, BLOCK), F32),
            pltpu.VMEM((frames, BLOCK), BF16),
            pltpu.SemaphoreType.DMA((count + 2,)),
        ],
        compiler_params=PARAMS,
        name="conv_product",
    )(core, block, low, high, taps, signal)


def merge_kernel(inverse_root, place_ref, parts_ref, carried_ref, right_ref, left_ref, *refs):
    out_refs, rows_ref = refs[:-1], refs[-1]
    sources, count, owned, features = parts_ref.shape
    place = place_ref[0]
    total = parts_ref[0].astype(F32)
    for index in range(1, sources):
        total = total + parts_ref[index].astype(F32)
    rows_ref[...] = total * inverse_root
    rows_ref[place] = rows_ref[place] + carried_ref[...]
    left = lax.dot_general(
        rows_ref[...].reshape(count * owned, features), right_ref[...], (((1,), (1,)), ((), ())),
        precision=HIGHEST, preferred_element_type=F32,
    )
    for index in range(count):
        top = left[index * owned : index * owned + owned // 2]
        low = left[index * owned + owned // 2 : (index + 1) * owned]
        packed = jnp.concatenate([top, low], axis=1)
        for copy in range(left_ref.shape[0]):
            left_ref[copy, index] = packed
    for shift, out_ref in enumerate(out_refs):
        out_ref[...] = rows_ref[lax.rem(place + shift, count)]


def term_kernel(replicas, left_parts_ref, *refs):
    row_refs, (merged_ref, left_ref, term_ref) = refs[:-3], refs[-3:]
    merged = row_refs[0][...]
    for ref in row_refs[1:]:
        merged = merged + ref[...]
    merged_ref[...] = merged
    packed = left_parts_ref[0]
    for index in range(1, left_parts_ref.shape[0]):
        packed = packed + left_parts_ref[index]
    rank = left_ref.shape[1]
    left = jnp.concatenate([packed[:, :rank], packed[:, rank:]], axis=0)
    left_ref[...] = left
    joined = jnp.concatenate([merged, jnp.zeros_like(left), left * (1.0 / replicas)], axis=1)
    term = lax.dot_general(
        left, joined, (((0,), (0,)), ((), ())), precision=HIGHEST, preferred_element_type=F32
    )
    for index in range(term_ref.shape[0]):
        term_ref[index] = term[2 * index : 2 * index + 2]


def total_kernel(parts_ref, total_ref):
    total = parts_ref[0]
    for index in range(1, parts_ref.shape[0]):
        total = total + parts_ref[index]
    for index in range(total_ref.shape[0]):
        total_ref[index] = total


def eliminate(rest, rank):
    done = []
    for start in range(0, rank, PANEL):
        row = lax.broadcasted_iota(jnp.int32, rest.shape, 0)
        first = rank + start
        columns = [
            jnp.broadcast_to(rest[:, first + j : first + j + 1], rest.shape) for j in range(PANEL)
        ]
        top = rest[:PANEL]
        scaled = []
        for j in range(PANEL):
            inverse = 1.0 / columns[j][j : j + 1]
            scaled.append(top[j : j + 1] * inverse)
            below = jnp.where(row > j, columns[j], 0.0)
            columns[j] = below
            for i in range(j + 1, PANEL):
                columns[i] = columns[i] - below * (columns[i][j : j + 1] * inverse)
            top = top - below[:PANEL] * scaled[j]
        done.append(top)
        rest = rest[PANEL:]
        if start + PANEL < rank:
            for j in range(PANEL):
                rest = rest - columns[j][PANEL:] * scaled[j]
    return jnp.concatenate(done, axis=0)


def finish_kernel(replicas, rows_ref, left_ref, merged_ref, right_ref, estimate_ref, error_ref, wide_ref):
    rank = left_ref.shape[1]
    features = merged_ref.shape[1]
    for index in range(rows_ref.shape[0]):
        wide_ref[2 * index : 2 * index + 2] = rows_ref[index]
    row = lax.broadcasted_iota(jnp.int32, (rank, 2 * rank), 0)
    lane = lax.broadcasted_iota(jnp.int32, (rank, 2 * rank), 1)
    work = eliminate(wide_ref[:, features:] + (row == lane).astype(F32), rank)
    pivots = jnp.sum(jnp.where(row + rank == lane, work, 0.0), axis=1, keepdims=True)
    inverse = (work * (1.0 / jnp.sqrt(pivots)))[:, :rank]
    dot = functools.partial(lax.dot_general, precision=HIGHEST, preferred_element_type=F32)
    right = dot(inverse, wide_ref[:, :features], (((1,), (0,)), ((), ()))) * (1.0 / replicas)
    right_ref[...] = right
    left_hat = dot(left_ref[...], inverse, (((1,), (1,)), ((), ())))
    estimate = dot(left_hat, right, (((1,), (0,)), ((), ())))
    estimate_ref[...] = estimate
    error_ref[...] = merged_ref[...] - estimate


def call(kernel, outs, *args, smem=0, scratch=()):
    spaces = [pltpu.SMEM] * smem + [pltpu.VMEM] * (len(args) - smem)
    return pl.pallas_call(
        kernel,
        in_specs=[pl.BlockSpec(memory_space=space) for space in spaces],
        out_shape=[jax.ShapeDtypeStruct(shape, F32) for shape in outs],
        scratch_shapes=list(scratch),
        compiler_params=PARAMS,
        name=getattr(kernel, "func", kernel).__name__,
    )(*args)


def exchange(block, axes):
    return lax.all_to_all(block, axes, 0, 0, tiled=True)


def local(gated_input, upstream, depth_kernel, carried_error, right_init):
    replicas = lax.axis_size(DP)
    contexts = lax.axis_size(CTX)
    block = gated_input[0]
    frames, channels = block.shape
    features = upstream.shape[2]
    rank = right_init.shape[1]
    owned = channels // contexts
    forward = [(i, i + 1) for i in range(contexts - 1)]
    backward = [(target, source) for source, target in forward]
    low = lax.ppermute(block[frames - RIM :], CTX, forward)
    high = lax.ppermute(block[:RIM], CTX, backward)
    core = lax.axis_index("c").reshape(1)
    keep, send = conv_product(core, block, low, high, depth_kernel, upstream[0])
    received = lax.ppermute(send, "c", [(0, 1), (1, 0)])
    pair_sum = (keep + received).astype(BF16)
    parts = exchange(pair_sum, "z")
    inverse_root = 1.0 / math.sqrt(frames * contexts)
    runs = lax.axis_size("y")
    row = (owned, features)
    left_parts, *shifted = call(
        functools.partial(merge_kernel, inverse_root),
        [(replicas, runs, owned // 2, 2 * rank)] + [row] * runs,
        lax.axis_index("y").reshape(1),
        parts,
        carried_error[0],
        right_init.T,
        smem=1,
        scratch=[pltpu.VMEM((runs, owned, features), F32)],
    )
    for shift in range(1, runs):
        shifted[shift] = lax.ppermute(
            shifted[shift], "y", [(i, (i + shift) % runs) for i in range(runs)]
        )
    left_parts = exchange(left_parts.reshape(replicas * runs, owned // 2, 2 * rank), ROWS)
    width = features + 2 * rank
    near, far = lax.axis_size(NEAR), lax.axis_size(FAR)
    pair = rank // near
    merged, left, term = call(
        functools.partial(term_kernel, replicas),
        [row, (owned, rank), (near, pair, width)],
        left_parts,
        *shifted,
    )
    (near_sum,) = call(total_kernel, [(far, pair, width)], exchange(term, NEAR))
    (far_sum,) = call(total_kernel, [(near, pair, width)], exchange(near_sum, FAR))
    right, estimate, error = call(
        functools.partial(finish_kernel, replicas),
        [(rank, features), row, row],
        exchange(far_sum, NEAR),
        left,
        merged,
        scratch=[pltpu.VMEM((rank, width), F32)],
    )
    return right.T, estimate, error[None]


def solution(mesh):
    wide = Mesh(mesh.devices.reshape(4, 2, 4, 8, 2), ("x", "h", "y", "z", "c"))
    return jax.shard_map(
        local,
        mesh=wide,
        in_specs=(P(DP, CTX, None), P(DP, CTX, None), P(), P(DP, CTX, None), P()),
        out_specs=(P(), P(CTX, None), P(DP, CTX, None)),
        check_vma=False,
    )
```

```python
import functools
import math

import jax
import jax.numpy as jnp
from jax import lax
from jax.experimental import pallas as pl
from jax.experimental.pallas import tpu as pltpu
from jax.sharding import Mesh, PartitionSpec as P

F32 = jnp.float32
BF16 = jnp.bfloat16
HIGHEST = lax.Precision.HIGHEST
DP = ("x", "h")
CTX = ("y", "z", "c")
CHIPS = ("y", "z")
NEAR = ("x", "z")
FAR = ("h", "y", "c")
RIM = 16
LANES = 128
TILE = 8
BLOCK = 512
STEP = 192
PANEL = 8
PARAMS = pltpu.CompilerParams(vmem_limit_bytes=48 << 20)


def conv_kernel(
    core_ref, block_hbm, low_ref, high_ref, taps_hbm, up_hbm, keep_ref, send_ref,
    block_ref, taps_ref, up_ref, wide_ref, sums_ref, weights_ref, act_ref, sems,
):
    frames, width = act_ref.shape
    count = block_ref.shape[0]
    rows = frames + 2 * RIM
    step = pl.program_id(0)

    def block_copy(index):
        cols = pl.ds(pl.multiple_of(index * width, width), width)
        return pltpu.make_async_copy(block_hbm.at[:, cols], block_ref.at[index], sems.at[index])

    taps_copy = pltpu.make_async_copy(taps_hbm, taps_ref, sems.at[count])
    up_copy = pltpu.make_async_copy(up_hbm, up_ref, sems.at[count + 1])

    @pl.when(step == 0)
    def _():
        block_copy(0).start()
        taps_copy.start()
        for index in range(1, count):
            block_copy(index).start()
        up_copy.start()
        taps_copy.wait()

    block_copy(step).wait()
    for group in range(width // LANES):
        cols = slice(LANES * group, LANES * (group + 1))
        tap_cols = pl.ds(pl.multiple_of(step * width + LANES * group, LANES), LANES)
        wide_ref[group, 0:RIM] = low_ref[:, cols].astype(F32)
        wide_ref[group, RIM : RIM + frames] = block_ref[step, :, cols].astype(F32)
        wide_ref[group, RIM + frames : rows] = high_ref[:, cols].astype(F32)
        sums_ref[group, 0 : rows - TILE] = wide_ref[group, 0 : rows - TILE] + wide_ref[group, TILE:rows]
        weights_ref[group, 0:1] = jnp.zeros((1, LANES), F32)
        weights_ref[group, 1:32] = taps_ref[:, tap_cols]
        weights_ref[group, 32:40] = weights_ref[group, 0:8] + weights_ref[group, 8:16]
        weights_ref[group, 40:48] = weights_ref[group, 16:24] + weights_ref[group, 24:32]

    pairs = STEP // (2 * TILE)
    for group in range(width // LANES):

        def chunk(index, _):
            base = pl.multiple_of(index * STEP, STEP)
            even, odd, both = [None] * (pairs + 1), [None] * pairs, [None] * pairs

            def add(totals, place, weight, value):
                term = weight * value
                totals[place] = term if totals[place] is None else totals[place] + term

            for shift in range(TILE):

                def weight(first):
                    return weights_ref[group, first + shift : first + shift + 1]

                def tiles(ref, first, number):
                    return [
                        ref[group, pl.ds(base + shift + TILE * (first + 2 * k), TILE)]
                        for k in range(number)
                    ]

                values = tiles(wide_ref, 0, pairs + 2)
                for k in range(pairs + 1):
                    if shift:
                        add(even, k, weight(0), values[k])
                    add(even, k, weight(16), values[k + 1])
                values = tiles(wide_ref, 1, pairs + 1)
                for k in range(pairs):
                    add(odd, k, weight(8), values[k])
                    add(odd, k, weight(24), values[k + 1])
                values = tiles(sums_ref, 1, pairs + 1)
                for k in range(pairs):
                    add(both, k, weight(32), values[k])
                    add(both, k, weight(40), values[k + 1])
            for k in range(pairs):
                total = jnp.concatenate(
                    [even[k] + odd[k], both[k] - (even[k + 1] + odd[k])], axis=0
                )
                half = 0.5 * total
                act_ref[
                    pl.ds(pl.multiple_of(base + 2 * TILE * k, 2 * TILE), 2 * TILE),
                    LANES * group : LANES * (group + 1),
                ] = (half + half * jnp.tanh(half)).astype(BF16)
            return 0

        lax.fori_loop(0, frames // STEP, chunk, 0)

    @pl.when(step == 0)
    def _():
        up_copy.wait()

    product = lax.dot_general(
        act_ref[...], up_ref[...], (((0,), (0,)), ((), ())), preferred_element_type=F32
    )
    pieces = product.reshape(width // 32, 2, 16, product.shape[1])
    first, second = pieces[:, 0], pieces[:, 1]

    @pl.when(core_ref[0] == 0)
    def _():
        keep_ref[...] = first
        send_ref[...] = second

    @pl.when(core_ref[0] == 1)
    def _():
        keep_ref[...] = second
        send_ref[...] = first


def conv_product(core, block, low, high, taps, signal):
    frames, channels = block.shape
    features = signal.shape[1]
    count = channels // BLOCK
    groups = BLOCK // LANES
    half = jax.ShapeDtypeStruct((channels // 32, 16, features), F32)
    rim = pl.BlockSpec((RIM, BLOCK), lambda i: (0, i))
    far = pl.BlockSpec(memory_space=pltpu.HBM)
    block, taps, signal = (
        pltpu.with_memory_space_constraint(array, pltpu.HBM) for array in (block, taps, signal)
    )
    return pl.pallas_call(
        conv_kernel,
        grid=(count,),
        in_specs=[pl.BlockSpec(memory_space=pltpu.SMEM), far, rim, rim, far, far],
        out_specs=[pl.BlockSpec((BLOCK // 32, 16, features), lambda i: (i, 0, 0))] * 2,
        out_shape=[half, half],
        scratch_shapes=[
            pltpu.VMEM((count, frames, BLOCK), BF16),
            pltpu.VMEM(taps.shape, F32),
            pltpu.VMEM(signal.shape, BF16),
            pltpu.VMEM((groups, frames + 2 * RIM, LANES), F32),
            pltpu.VMEM((groups, frames + 2 * RIM, LANES), F32),
            pltpu.VMEM((groups, 48, LANES), F32),
            pltpu.VMEM((frames, BLOCK), BF16),
            pltpu.SemaphoreType.DMA((count + 2,)),
        ],
        compiler_params=PARAMS,
        name="conv_product",
    )(core, block, low, high, taps, signal)


def pair_kernel(keep_ref, received_ref, pair_ref):
    pair_ref[...] = (keep_ref[...] + received_ref[...]).astype(BF16)


def merge_kernel(inverse_root, parts_ref, carried_ref, right_ref, merged_ref, left_ref):
    total = parts_ref[0].astype(F32)
    for index in range(1, parts_ref.shape[0]):
        total = total + parts_ref[index].astype(F32)
    merged = total * inverse_root + carried_ref[...]
    merged_ref[...] = merged
    left = lax.dot_general(
        merged, right_ref[...], (((1,), (1,)), ((), ())), precision=HIGHEST, preferred_element_type=F32
    )
    middle = left.shape[0] // 2
    packed = jnp.concatenate([left[:middle], left[middle:]], axis=1)
    for index in range(left_ref.shape[0]):
        left_ref[index] = packed


def term_kernel(parts_ref, merged_ref, left_ref, term_ref):
    packed = parts_ref[0]
    for index in range(1, parts_ref.shape[0]):
        packed = packed + parts_ref[index]
    rank = left_ref.shape[1]
    left = jnp.concatenate([packed[:, :rank], packed[:, rank:]], axis=0)
    left_ref[...] = left
    share = left * (1.0 / parts_ref.shape[0])
    joined = jnp.concatenate([merged_ref[...], jnp.zeros_like(left), share], axis=1)
    term = lax.dot_general(
        left, joined, (((0,), (0,)), ((), ())), precision=HIGHEST, preferred_element_type=F32
    )
    for index in range(term_ref.shape[0]):
        term_ref[index] = term[2 * index : 2 * index + 2]


def total_kernel(parts_ref, total_ref):
    total = parts_ref[0]
    for index in range(1, parts_ref.shape[0]):
        total = total + parts_ref[index]
    for index in range(total_ref.shape[0]):
        total_ref[index] = total


def eliminate(rest, rank):
    done = []
    for start in range(0, rank, PANEL):
        row = lax.broadcasted_iota(jnp.int32, rest.shape, 0)
        first = rank + start
        columns = [
            jnp.broadcast_to(rest[:, first + j : first + j + 1], rest.shape) for j in range(PANEL)
        ]
        top = rest[:PANEL]
        scaled = []
        for j in range(PANEL):
            inverse = 1.0 / columns[j][j : j + 1]
            scaled.append(top[j : j + 1] * inverse)
            below = jnp.where(row > j, columns[j], 0.0)
            columns[j] = below
            for i in range(j + 1, PANEL):
                columns[i] = columns[i] - below * (columns[i][j : j + 1] * inverse)
            top = top - below[:PANEL] * scaled[j]
        done.append(top)
        rest = rest[PANEL:]
        if start + PANEL < rank:
            for j in range(PANEL):
                rest = rest - columns[j][PANEL:] * scaled[j]
    return jnp.concatenate(done, axis=0)


def finish_kernel(replicas, rows_ref, left_ref, merged_ref, right_ref, estimate_ref, error_ref, wide_ref):
    rank = left_ref.shape[1]
    features = merged_ref.shape[1]
    for index in range(rows_ref.shape[0]):
        wide_ref[2 * index : 2 * index + 2] = rows_ref[index]
    row = lax.broadcasted_iota(jnp.int32, (rank, 2 * rank), 0)
    lane = lax.broadcasted_iota(jnp.int32, (rank, 2 * rank), 1)
    work = eliminate(wide_ref[:, features:] + (row == lane).astype(F32), rank)
    pivots = jnp.sum(jnp.where(row + rank == lane, work, 0.0), axis=1, keepdims=True)
    inverse = (work * (1.0 / jnp.sqrt(pivots)))[:, :rank]
    dot = functools.partial(lax.dot_general, precision=HIGHEST, preferred_element_type=F32)
    right = dot(inverse, wide_ref[:, :features], (((1,), (0,)), ((), ()))) * (1.0 / replicas)
    right_ref[...] = right
    left_hat = dot(left_ref[...], inverse, (((1,), (1,)), ((), ())))
    estimate = dot(left_hat, right, (((1,), (0,)), ((), ())))
    estimate_ref[...] = estimate
    error_ref[...] = merged_ref[...] - estimate


def call(kernel, outs, *args, scratch=()):
    return pl.pallas_call(
        kernel,
        out_shape=[jax.ShapeDtypeStruct(out, F32) if isinstance(out, tuple) else out for out in outs],
        scratch_shapes=list(scratch),
        compiler_params=PARAMS,
        name=getattr(kernel, "func", kernel).__name__,
    )(*args)


def exchange(block, axes):
    return lax.all_to_all(block, axes, 0, 0, tiled=True)


def local(gated_input, upstream, depth_kernel, carried_error, right_init):
    replicas = lax.axis_size(DP)
    contexts = lax.axis_size(CTX)
    block = gated_input[0]
    frames, channels = block.shape
    features = upstream.shape[2]
    rank = right_init.shape[1]
    owned = channels // contexts
    forward = [(i, i + 1) for i in range(contexts - 1)]
    backward = [(target, source) for source, target in forward]
    low = lax.ppermute(block[frames - RIM :], CTX, forward)
    high = lax.ppermute(block[:RIM], CTX, backward)
    core = lax.axis_index("c").reshape(1)
    keep, send = conv_product(core, block, low, high, depth_kernel, upstream[0])
    received = lax.ppermute(send, "c", [(0, 1), (1, 0)])
    (pair_sum,) = call(pair_kernel, [pltpu.VMEM(keep.shape, BF16)], keep, received)
    inverse_root = 1.0 / math.sqrt(frames * contexts)
    row = (owned, features)
    merged, left_parts = call(
        functools.partial(merge_kernel, inverse_root),
        [row, pltpu.VMEM((replicas, owned // 2, 2 * rank), F32)],
        exchange(pair_sum, CHIPS),
        carried_error[0],
        right_init.T,
    )
    width = features + 2 * rank
    near, far = lax.axis_size(NEAR), lax.axis_size(FAR)
    near_form = pltpu.VMEM((near, rank // near, width), F32)
    far_form = pltpu.VMEM((far, rank // near, width), F32)
    left, term = call(term_kernel, [(owned, rank), near_form], exchange(left_parts, DP), merged)
    (near_sum,) = call(total_kernel, [far_form], exchange(term, NEAR))
    (far_sum,) = call(total_kernel, [near_form], exchange(near_sum, FAR))
    right, estimate, error = call(
        functools.partial(finish_kernel, replicas),
        [(rank, features), row, row],
        exchange(far_sum, NEAR),
        left,
        merged,
        scratch=[pltpu.VMEM((rank, width), F32)],
    )
    return right.T, estimate, error[None]


def solution(mesh):
    wide = Mesh(mesh.devices.reshape(4, 2, 4, 8, 2), ("x", "h", "y", "z", "c"))
    return jax.shard_map(
        local,
        mesh=wide,
        in_specs=(P(DP, CTX, None), P(DP, CTX, None), P(), P(DP, CTX, None), P()),
        out_specs=(P(), P(CTX, None), P(DP, CTX, None)),
        check_vma=False,
    )
```

```python
import functools
import math

import jax
import jax.numpy as jnp
from jax import lax
from jax.experimental import pallas as pl
from jax.experimental.pallas import tpu as pltpu
from jax.sharding import Mesh, PartitionSpec as P

F32 = jnp.float32
BF16 = jnp.bfloat16
HIGHEST = lax.Precision.HIGHEST
DP = ("x", "h")
CTX = ("y", "z", "c")
NEAR = ("x", "z")
FAR = ("h", "y", "c")
RIM = 16
LANES = 128
TILE = 8
STEP = 256
PANEL = 16
PARAMS = pltpu.CompilerParams(vmem_limit_bytes=48 << 20)


def conv_kernel(
    core_ref, block_hbm, other_ref, near_ref, far_ref, taps_hbm, act_ref,
    block_ref, taps_ref, wide_ref, sums_ref, weights_ref, sems,
):
    count, frames, width = block_ref.shape
    rows = 2 * frames + 2 * RIM
    core = core_ref[0]
    lane = lax.broadcasted_iota(jnp.int32, (1, LANES), 1)
    first = lax.rem(lane // 16, 2) == core_ref[1]
    own = pl.multiple_of(RIM + frames * core, RIM)
    partner = pl.multiple_of(RIM + frames * (1 - core), RIM)
    pairs = STEP // (2 * TILE)

    def block_copy(index):
        cols = pl.ds(pl.multiple_of(index * width, width), width)
        return pltpu.make_async_copy(block_hbm.at[:, cols], block_ref.at[index], sems.at[index])

    def picked(value):
        value = value.astype(F32)
        return jnp.where(first, value[:, :LANES], value[:, LANES:])

    taps_copy = pltpu.make_async_copy(taps_hbm, taps_ref, sems.at[count])
    for index in range(count):
        block_copy(index).start()
        if index == 0:
            taps_copy.start()

    def group(step, _):
        cols = pl.ds(pl.multiple_of(step * width, width), width)
        out_cols = pl.ds(pl.multiple_of(step * LANES, LANES), LANES)
        near, far = picked(near_ref[:, cols]), picked(far_ref[:, cols])
        wide_ref[0:RIM] = jnp.where(core == 0, near, far)
        wide_ref[rows - RIM : rows] = jnp.where(core == 0, far, near)
        wide_ref[pl.ds(partner, frames)] = picked(other_ref[:, cols])

        @pl.when(step == 0)
        def _():
            taps_copy.wait()

        weights_ref[0:1] = jnp.zeros((1, LANES), F32)
        weights_ref[1:32] = picked(taps_ref[:, cols])
        weights_ref[32:40] = weights_ref[0:8] + weights_ref[8:16]
        weights_ref[40:48] = weights_ref[16:24] + weights_ref[24:32]
        block_copy(step).wait()
        wide_ref[pl.ds(own, frames)] = picked(block_ref[step])
        sums_ref[0 : rows - TILE] = wide_ref[0 : rows - TILE] + wide_ref[TILE:rows]

        def chunk(index, _):
            base = pl.multiple_of(index * STEP, STEP)
            even, odd, both = [None] * (pairs + 1), [None] * pairs, [None] * pairs

            def add(totals, place, weight, value):
                term = weight * value
                totals[place] = term if totals[place] is None else totals[place] + term

            for shift in range(TILE):

                def weight(row):
                    return weights_ref[row + shift : row + shift + 1]

                def tiles(ref, start, number):
                    return [
                        ref[pl.ds(base + shift + TILE * (start + 2 * k), TILE)] for k in range(number)
                    ]

                values = tiles(wide_ref, 0, pairs + 2)
                for k in range(pairs + 1):
                    if shift:
                        add(even, k, weight(0), values[k])
                    add(even, k, weight(16), values[k + 1])
                values = tiles(wide_ref, 1, pairs + 1)
                for k in range(pairs):
                    add(odd, k, weight(8), values[k])
                    add(odd, k, weight(24), values[k + 1])
                values = tiles(sums_ref, 1, pairs + 1)
                for k in range(pairs):
                    add(both, k, weight(32), values[k])
                    add(both, k, weight(40), values[k + 1])
            for k in range(pairs):
                total = jnp.concatenate(
                    [even[k] + odd[k], both[k] - (even[k + 1] + odd[k])], axis=0
                )
                half = 0.5 * total
                place = pl.ds(pl.multiple_of(base + 2 * TILE * k, 2 * TILE), 2 * TILE)
                act_ref[place, out_cols] = (half + half * jnp.tanh(half)).astype(BF16)
            return 0

        lax.fori_loop(0, 2 * frames // STEP, chunk, 0)
        return 0

    lax.fori_loop(0, count, group, 0)


def activation(core, block, other, near, far, taps):
    frames, channels = block.shape
    width = 2 * LANES
    count = channels // width
    rows = 2 * frames + 2 * RIM
    smem, vmem, hbm = (
        pl.BlockSpec(memory_space=space) for space in (pltpu.SMEM, pltpu.VMEM, pltpu.HBM)
    )
    block, taps = (pltpu.with_memory_space_constraint(array, pltpu.HBM) for array in (block, taps))
    return pl.pallas_call(
        conv_kernel,
        in_specs=[smem, hbm, vmem, vmem, vmem, hbm],
        out_specs=vmem,
        out_shape=pltpu.VMEM((2 * frames, channels // 2), BF16),
        scratch_shapes=[
            pltpu.VMEM((count, frames, width), BF16),
            pltpu.VMEM(taps.shape, F32),
            pltpu.VMEM((rows, LANES), F32),
            pltpu.VMEM((rows, LANES), F32),
            pltpu.VMEM((48, LANES), F32),
            pltpu.SemaphoreType.DMA((count + 1,)),
        ],
        compiler_params=PARAMS,
        name="activation",
    )(core, block, other, near, far, taps)


def product_kernel(core_ref, act_ref, own_ref, other_ref, product_ref):
    frames = own_ref.shape[0]
    core = core_ref[0]

    def part(first, signal_ref):
        act = act_ref[pl.ds(pl.multiple_of(first, frames), frames)]
        return lax.dot_general(
            act, signal_ref[...], (((0,), (0,)), ((), ())), preferred_element_type=F32
        )

    total = part(frames * core, own_ref) + part(frames * (1 - core), other_ref)
    blocks, _, quarter, owned, features = product_ref.shape
    pieces = total.reshape(blocks, quarter, 2, owned, features).astype(BF16)
    for parity in range(2):
        product_ref[:, lax.rem(parity + core_ref[1], 2)] = pieces[:, :, parity]


def merge_kernel(inverse_root, parts_ref, carried_ref, right_ref, merged_ref, left_ref):
    total = parts_ref[0].astype(F32)
    for index in range(1, parts_ref.shape[0]):
        total = total + parts_ref[index].astype(F32)
    merged = total * inverse_root + carried_ref[...]
    merged_ref[...] = merged
    left = lax.dot_general(
        merged, right_ref[...], (((1,), (1,)), ((), ())), precision=HIGHEST, preferred_element_type=F32
    )
    middle = left.shape[0] // 2
    packed = jnp.concatenate([left[:middle], left[middle:]], axis=1)
    for index in range(left_ref.shape[0]):
        left_ref[index] = packed


def term_kernel(parts_ref, merged_ref, left_ref, term_ref):
    packed = parts_ref[0]
    for index in range(1, parts_ref.shape[0]):
        packed = packed + parts_ref[index]
    rank = left_ref.shape[1]
    left = jnp.concatenate([packed[:, :rank], packed[:, rank:]], axis=0)
    left_ref[...] = left
    share = left * (1.0 / parts_ref.shape[0])
    joined = jnp.concatenate([merged_ref[...], jnp.zeros_like(left), share], axis=1)
    term = lax.dot_general(
        left, joined, (((0,), (0,)), ((), ())), precision=HIGHEST, preferred_element_type=F32
    )
    for index in range(term_ref.shape[0]):
        term_ref[index] = term[2 * index : 2 * index + 2]


def total_kernel(parts_ref, total_ref):
    total = parts_ref[0]
    for index in range(1, parts_ref.shape[0]):
        total = total + parts_ref[index]
    for index in range(total_ref.shape[0]):
        total_ref[index] = total


def eliminate(rest, rank):
    done = []
    for start in range(0, rank, PANEL):
        row = lax.broadcasted_iota(jnp.int32, rest.shape, 0)
        first = rank + start
        columns = [
            jnp.broadcast_to(rest[:, first + j : first + j + 1], rest.shape) for j in range(PANEL)
        ]
        top = rest[:PANEL]
        scaled = []
        for j in range(PANEL):
            inverse = 1.0 / columns[j][j : j + 1]
            scaled.append(top[j : j + 1] * inverse)
            below = jnp.where(row > j, columns[j], 0.0)
            columns[j] = below
            for i in range(j + 1, PANEL):
                columns[i] = columns[i] - below * (columns[i][j : j + 1] * inverse)
            top = top - below[:PANEL] * scaled[j]
        done.append(top)
        rest = rest[PANEL:]
        if start + PANEL < rank:
            for j in range(PANEL):
                rest = rest - columns[j][PANEL:] * scaled[j]
    return jnp.concatenate(done, axis=0)


def finish_kernel(replicas, rows_ref, left_ref, merged_ref, right_ref, estimate_ref, error_ref, wide_ref):
    rank = left_ref.shape[1]
    features = merged_ref.shape[1]
    for index in range(rows_ref.shape[0]):
        wide_ref[2 * index : 2 * index + 2] = rows_ref[index]
    row = lax.broadcasted_iota(jnp.int32, (rank, 2 * rank), 0)
    lane = lax.broadcasted_iota(jnp.int32, (rank, 2 * rank), 1)
    work = eliminate(wide_ref[:, features:] + (row == lane).astype(F32), rank)
    pivots = jnp.sum(jnp.where(row + rank == lane, work, 0.0), axis=1, keepdims=True)
    inverse = (work * (1.0 / jnp.sqrt(pivots)))[:, :rank]
    dot = functools.partial(lax.dot_general, precision=HIGHEST, preferred_element_type=F32)
    right = dot(inverse, wide_ref[:, :features], (((1,), (0,)), ((), ()))) * (1.0 / replicas)
    right_ref[...] = right
    left_hat = dot(left_ref[...], inverse, (((1,), (1,)), ((), ())))
    estimate = dot(left_hat, right, (((1,), (0,)), ((), ())))
    estimate_ref[...] = estimate
    error_ref[...] = merged_ref[...] - estimate


def call(kernel, outs, *args, smem=0, scratch=()):
    spaces = [pltpu.SMEM] * smem + [pltpu.VMEM] * (len(args) - smem)
    return pl.pallas_call(
        kernel,
        in_specs=[pl.BlockSpec(memory_space=space) for space in spaces],
        out_shape=[jax.ShapeDtypeStruct(out, F32) if isinstance(out, tuple) else out for out in outs],
        scratch_shapes=list(scratch),
        compiler_params=PARAMS,
        name=getattr(kernel, "func", kernel).__name__,
    )(*args)


def exchange(block, axes, groups=None):
    return lax.all_to_all(block, axes, 0, 0, tiled=True, axis_index_groups=groups)


def local(gated_input, upstream, depth_kernel, carried_error, right_init):
    replicas = lax.axis_size(DP)
    contexts = lax.axis_size(CTX)
    block = gated_input[0]
    frames, channels = block.shape
    features = upstream.shape[2]
    rank = right_init.shape[1]
    owned = channels // contexts
    core = lax.axis_index("c")
    swap = [(0, 1), (1, 0)]
    ends = lax.dynamic_slice_in_dim(block, core * (frames - RIM), RIM, axis=0)
    one = [(i, i + 1 if i % 2 else i - 1) for i in range(1, contexts - 1)]
    two = [(i, i + 2 if i % 2 else i - 2) for i in range(1, contexts - 1)]
    ends, block = lax.optimization_barrier((ends, block))
    near = lax.ppermute(ends, CTX, one)
    far = lax.ppermute(ends, CTX, two)
    other = lax.ppermute(block, "c", swap)
    signal = upstream[0]
    other_signal = lax.ppermute(signal, "c", swap)
    depth = lax.axis_size("z")
    side = [(2 * z) // depth for z in range(depth)]
    teams = [
        [2 * chip + (team + side[chip % depth]) % 2 for chip in range(contexts // 2)]
        for team in range(2)
    ]
    team = lax.rem(core + (2 * lax.axis_index("z")) // depth, 2)
    core = jnp.stack([core, team])
    act = activation(core, block, other, near, far, depth_kernel)
    (product,) = call(
        product_kernel,
        [pltpu.VMEM((channels // 256, 2, 4, owned, features), BF16)],
        core,
        act,
        signal,
        other_signal,
        smem=1,
    )
    inverse_root = 1.0 / math.sqrt(frames * contexts)
    row = (owned, features)
    merged, left_parts = call(
        functools.partial(merge_kernel, inverse_root),
        [row, pltpu.VMEM((replicas, owned // 2, 2 * rank), F32)],
        exchange(product.reshape(channels // 32, owned, features), CTX, teams),
        carried_error[0],
        right_init.T,
    )
    width = features + 2 * rank
    near, far = lax.axis_size(NEAR), lax.axis_size(FAR)
    near_form = pltpu.VMEM((near, rank // near, width), F32)
    far_form = pltpu.VMEM((far, rank // near, width), F32)
    left, term = call(term_kernel, [(owned, rank), near_form], exchange(left_parts, DP), merged)
    (near_sum,) = call(total_kernel, [far_form], exchange(term, NEAR))
    (far_sum,) = call(total_kernel, [near_form], exchange(near_sum, FAR))
    right, estimate, error = call(
        functools.partial(finish_kernel, replicas),
        [(rank, features), row, row],
        exchange(far_sum, NEAR),
        left,
        merged,
        scratch=[pltpu.VMEM((rank, width), F32)],
    )
    return right.T, estimate, error[None]


def solution(mesh):
    wide = Mesh(mesh.devices.reshape(4, 2, 4, 8, 2), ("x", "h", "y", "z", "c"))
    return jax.shard_map(
        local,
        mesh=wide,
        in_specs=(P(DP, CTX, None), P(DP, CTX, None), P(), P(DP, CTX, None), P()),
        out_specs=(P(), P(CTX, None), P(DP, CTX, None)),
        check_vma=False,
    )
```

```python
import functools
import math

import jax
import jax.numpy as jnp
from jax import lax
from jax.experimental import pallas as pl
from jax.experimental.pallas import tpu as pltpu
from jax.sharding import Mesh, PartitionSpec as P

F32 = jnp.float32
BF16 = jnp.bfloat16
HIGHEST = lax.Precision.HIGHEST
DP = ("x", "h")
CTX = ("y", "z", "c")
NEAR = ('y', 'c')
FAR = ('z',)
RIM = 16
LANES = 128
TILE = 8
STEP = 256
PANEL = 16
PARAMS = pltpu.CompilerParams(vmem_limit_bytes=48 << 20)


def conv_kernel(
    place_ref, block_hbm, other_ref, near_ref, far_ref, taps_hbm, act_ref,
    block_ref, taps_ref, wide_ref, sums_ref, weights_ref, sems,
):
    count, frames, width = block_ref.shape
    rows = 2 * frames + 2 * RIM
    core = place_ref[0]
    lane = lax.broadcasted_iota(jnp.int32, (1, LANES), 1)
    first = lax.rem(lane // 16, 2) == place_ref[1]
    own = pl.multiple_of(RIM + frames * core, RIM)
    partner = pl.multiple_of(RIM + frames * (1 - core), RIM)
    pairs = STEP // (2 * TILE)

    def block_copy(index):
        cols = pl.ds(pl.multiple_of(index * width, width), width)
        return pltpu.make_async_copy(block_hbm.at[:, cols], block_ref.at[index], sems.at[index])

    def picked(value):
        value = value.astype(F32)
        return jnp.where(first, value[:, :LANES], value[:, LANES:])

    taps_copy = pltpu.make_async_copy(taps_hbm, taps_ref, sems.at[count])
    for index in range(count):
        block_copy(index).start()
        if index == 0:
            taps_copy.start()

    def group(step, _):
        cols = pl.ds(pl.multiple_of(step * width, width), width)
        out_cols = pl.ds(pl.multiple_of(step * LANES, LANES), LANES)
        near, far = picked(near_ref[:, cols]), picked(far_ref[:, cols])
        wide_ref[0:RIM] = jnp.where(core == 0, near, far)
        wide_ref[rows - RIM : rows] = jnp.where(core == 0, far, near)
        wide_ref[pl.ds(partner, frames)] = picked(other_ref[:, cols])

        @pl.when(step == 0)
        def _():
            taps_copy.wait()

        weights_ref[0:1] = jnp.zeros((1, LANES), F32)
        weights_ref[1:32] = picked(taps_ref[:, cols])
        weights_ref[32:40] = weights_ref[0:8] + weights_ref[8:16]
        weights_ref[40:48] = weights_ref[16:24] + weights_ref[24:32]
        block_copy(step).wait()
        wide_ref[pl.ds(own, frames)] = picked(block_ref[step])
        sums_ref[0 : rows - TILE] = wide_ref[0 : rows - TILE] + wide_ref[TILE:rows]

        def chunk(index, _):
            base = pl.multiple_of(index * STEP, STEP)
            even, odd, both = [None] * (pairs + 1), [None] * pairs, [None] * pairs

            def add(totals, place, weight, value):
                term = weight * value
                totals[place] = term if totals[place] is None else totals[place] + term

            for shift in range(TILE):

                def weight(row):
                    return weights_ref[row + shift : row + shift + 1]

                def tiles(ref, start, number):
                    return [
                        ref[pl.ds(base + shift + TILE * (start + 2 * k), TILE)] for k in range(number)
                    ]

                values = tiles(wide_ref, 0, pairs + 2)
                for k in range(pairs + 1):
                    if shift:
                        add(even, k, weight(0), values[k])
                    add(even, k, weight(16), values[k + 1])
                values = tiles(wide_ref, 1, pairs + 1)
                for k in range(pairs):
                    add(odd, k, weight(8), values[k])
                    add(odd, k, weight(24), values[k + 1])
                values = tiles(sums_ref, 1, pairs + 1)
                for k in range(pairs):
                    add(both, k, weight(32), values[k])
                    add(both, k, weight(40), values[k + 1])
            for k in range(pairs):
                total = jnp.concatenate(
                    [even[k] + odd[k], both[k] - (even[k + 1] + odd[k])], axis=0
                )
                half = 0.5 * total
                place = pl.ds(pl.multiple_of(base + 2 * TILE * k, 2 * TILE), 2 * TILE)
                act_ref[place, out_cols] = (half + half * jnp.tanh(half)).astype(BF16)
            return 0

        lax.fori_loop(0, 2 * frames // STEP, chunk, 0)
        return 0

    lax.fori_loop(0, count, group, 0)


def activation(place, block, other, near, far, taps):
    frames, channels = block.shape
    width = 2 * LANES
    count = channels // width
    rows = 2 * frames + 2 * RIM
    smem, vmem, hbm = (
        pl.BlockSpec(memory_space=space) for space in (pltpu.SMEM, pltpu.VMEM, pltpu.HBM)
    )
    block, taps = (pltpu.with_memory_space_constraint(array, pltpu.HBM) for array in (block, taps))
    return pl.pallas_call(
        conv_kernel,
        in_specs=[smem, hbm, vmem, vmem, vmem, hbm],
        out_specs=vmem,
        out_shape=pltpu.VMEM((2 * frames, channels // 2), BF16),
        scratch_shapes=[
            pltpu.VMEM((count, frames, width), BF16),
            pltpu.VMEM(taps.shape, F32),
            pltpu.VMEM((rows, LANES), F32),
            pltpu.VMEM((rows, LANES), F32),
            pltpu.VMEM((48, LANES), F32),
            pltpu.SemaphoreType.DMA((count + 1,)),
        ],
        compiler_params=PARAMS,
        name="activation",
    )(place, block, other, near, far, taps)


def product_kernel(place_ref, act_ref, own_ref, other_ref, product_ref):
    frames = own_ref.shape[0]
    core = place_ref[0]

    def part(first, signal_ref):
        act = act_ref[pl.ds(pl.multiple_of(first, frames), frames)]
        return lax.dot_general(
            act, signal_ref[...], (((0,), (0,)), ((), ())), preferred_element_type=F32
        )

    total = part(frames * core, own_ref) + part(frames * (1 - core), other_ref)
    blocks, _, quarter, owned, features = product_ref.shape
    pieces = total.reshape(blocks, quarter, 2, owned, features).astype(BF16)
    for parity in range(2):
        product_ref[:, lax.rem(parity + place_ref[1], 2)] = pieces[:, :, parity]


def merge_kernel(inverse_root, parts_ref, carried_ref, right_ref, merged_ref, shares_ref):
    total = parts_ref[0].astype(F32)
    for index in range(1, parts_ref.shape[0]):
        total = total + parts_ref[index].astype(F32)
    merged = total * inverse_root + carried_ref[...]
    merged_ref[...] = merged
    left = lax.dot_general(
        merged, right_ref[...], (((1,), (1,)), ((), ())), precision=HIGHEST, preferred_element_type=F32
    )
    owned = left.shape[0]
    packed = jnp.concatenate([left[: owned // 2], left[owned // 2 :]], axis=1)
    for index in range(shares_ref.shape[0]):
        shares_ref[index, :owned] = merged[:, LANES * index : LANES * (index + 1)]
        shares_ref[index, owned:] = packed


def term_kernel(place_ref, parts_ref, left_ref, term_ref, gram_ref):
    total = parts_ref[0]
    for index in range(1, parts_ref.shape[0]):
        total = total + parts_ref[index]
    owned, rank = left_ref.shape
    packed = total[owned:]
    left = jnp.concatenate([packed[:, :rank], packed[:, rank:]], axis=0)
    left_ref[...] = left
    dot = functools.partial(
        lax.dot_general,
        dimension_numbers=(((0,), (0,)), ((), ())),
        precision=HIGHEST,
        preferred_element_type=F32,
    )
    term = dot(left, total[:owned])
    gram_ref[...] = dot(left, jnp.concatenate([jnp.zeros_like(left), left], axis=1))
    gram = gram_ref[pl.ds(pl.multiple_of(TILE * place_ref[2], TILE), TILE)]
    for index in range(term_ref.shape[0]):
        term_ref[index, :rank] = term
        term_ref[index, rank:] = gram


def total_kernel(parts_ref, total_ref):
    total = parts_ref[0]
    for index in range(1, parts_ref.shape[0]):
        total = total + parts_ref[index]
    for index in range(total_ref.shape[0]):
        total_ref[index] = total


def eliminate(rest, rank):
    done = []
    for start in range(0, rank, PANEL):
        row = lax.broadcasted_iota(jnp.int32, rest.shape, 0)
        first = rank + start
        columns = [
            jnp.broadcast_to(rest[:, first + j : first + j + 1], rest.shape) for j in range(PANEL)
        ]
        top = rest[:PANEL]
        scaled = []
        for j in range(PANEL):
            inverse = 1.0 / columns[j][j : j + 1]
            scaled.append(top[j : j + 1] * inverse)
            below = jnp.where(row > j, columns[j], 0.0)
            columns[j] = below
            for i in range(j + 1, PANEL):
                columns[i] = columns[i] - below * (columns[i][j : j + 1] * inverse)
            top = top - below[:PANEL] * scaled[j]
        done.append(top)
        rest = rest[PANEL:]
        if start + PANEL < rank:
            for j in range(PANEL):
                rest = rest - columns[j][PANEL:] * scaled[j]
    return jnp.concatenate(done, axis=0)


def finish_kernel(replicas, rows_ref, left_ref, merged_ref, right_ref, estimate_ref, error_ref, wide_ref):
    rank = left_ref.shape[1]
    features = merged_ref.shape[1]
    for index in range(rows_ref.shape[0]):
        wide_ref[:, LANES * index : LANES * (index + 1)] = rows_ref[index, :rank]
        wide_ref[TILE * index : TILE * (index + 1), features:] = rows_ref[index, rank:]
    row = lax.broadcasted_iota(jnp.int32, (rank, 2 * rank), 0)
    lane = lax.broadcasted_iota(jnp.int32, (rank, 2 * rank), 1)
    work = eliminate(wide_ref[:, features:] + (row == lane).astype(F32), rank)
    pivots = jnp.sum(jnp.where(row + rank == lane, work, 0.0), axis=1, keepdims=True)
    inverse = (work * (1.0 / jnp.sqrt(pivots)))[:, :rank]
    dot = functools.partial(lax.dot_general, precision=HIGHEST, preferred_element_type=F32)
    right = dot(inverse, wide_ref[:, :features], (((1,), (0,)), ((), ()))) * (1.0 / replicas)
    right_ref[...] = right
    left_hat = dot(left_ref[...], inverse, (((1,), (1,)), ((), ())))
    estimate = dot(left_hat, right, (((1,), (0,)), ((), ())))
    estimate_ref[...] = estimate
    error_ref[...] = merged_ref[...] - estimate


def call(kernel, outs, *args, smem=0, scratch=()):
    spaces = [pltpu.SMEM] * smem + [pltpu.VMEM] * (len(args) - smem)
    return pl.pallas_call(
        kernel,
        in_specs=[pl.BlockSpec(memory_space=space) for space in spaces],
        out_shape=[jax.ShapeDtypeStruct(out, F32) if isinstance(out, tuple) else out for out in outs],
        scratch_shapes=list(scratch),
        compiler_params=PARAMS,
        name=getattr(kernel, "func", kernel).__name__,
    )(*args)


def exchange(block, axes, groups=None):
    return lax.all_to_all(block, axes, 0, 0, tiled=True, axis_index_groups=groups)


def local(gated_input, upstream, depth_kernel, carried_error, right_init):
    replicas = lax.axis_size(DP)
    contexts = lax.axis_size(CTX)
    block = gated_input[0]
    frames, channels = block.shape
    features = upstream.shape[2]
    rank = right_init.shape[1]
    owned = channels // contexts
    core = lax.axis_index("c")
    swap = [(0, 1), (1, 0)]
    ends = lax.dynamic_slice_in_dim(block, core * (frames - RIM), RIM, axis=0)
    one = [(i, i + 1 if i % 2 else i - 1) for i in range(1, contexts - 1)]
    two = [(i, i + 2 if i % 2 else i - 2) for i in range(1, contexts - 1)]
    ends, block = lax.optimization_barrier((ends, block))
    near = lax.ppermute(ends, CTX, one)
    far = lax.ppermute(ends, CTX, two)
    other = lax.ppermute(block, "c", swap)
    signal = upstream[0]
    other_signal = lax.ppermute(signal, "c", swap)
    depth = lax.axis_size("z")
    side = [(2 * z) // depth for z in range(depth)]
    teams = [
        [2 * chip + (team + side[chip % depth]) % 2 for chip in range(contexts // 2)]
        for team in range(2)
    ]
    team = lax.rem(core + (2 * lax.axis_index("z")) // depth, 2)
    place = jnp.stack([core, team, lax.axis_index(DP)])
    act = activation(place, block, other, near, far, depth_kernel)
    (product,) = call(
        product_kernel,
        [pltpu.VMEM((channels // 256, 2, 4, owned, features), BF16)],
        place,
        act,
        signal,
        other_signal,
        smem=1,
    )
    inverse_root = 1.0 / math.sqrt(frames * contexts)
    row = (owned, features)
    merged, shares = call(
        functools.partial(merge_kernel, inverse_root),
        [row, pltpu.VMEM((replicas, owned + owned // 2, LANES), F32)],
        exchange(product.reshape(channels // 32, owned, features), CTX, teams),
        carried_error[0],
        right_init.T,
    )
    near, far = lax.axis_size(NEAR), lax.axis_size(FAR)
    size = (rank + TILE, LANES)
    left, term = call(
        term_kernel,
        [(owned, rank), pltpu.VMEM((near, *size), F32)],
        place,
        exchange(shares, DP),
        smem=1,
        scratch=[pltpu.VMEM((rank, LANES), F32)],
    )
    (near_sum,) = call(total_kernel, [pltpu.VMEM((far, *size), F32)], exchange(term, NEAR))
    (far_sum,) = call(total_kernel, [pltpu.VMEM((replicas, *size), F32)], exchange(near_sum, FAR))
    right, estimate, error = call(
        functools.partial(finish_kernel, replicas),
        [(rank, features), row, row],
        exchange(far_sum, DP),
        left,
        merged,
        scratch=[pltpu.VMEM((rank, features + 2 * rank), F32)],
    )
    return right.T, estimate, error[None]


def solution(mesh):
    wide = Mesh(mesh.devices.reshape(4, 2, 4, 8, 2), ("x", "h", "y", "z", "c"))
    return jax.shard_map(
        local,
        mesh=wide,
        in_specs=(P(DP, CTX, None), P(DP, CTX, None), P(), P(DP, CTX, None), P()),
        out_specs=(P(), P(CTX, None), P(DP, CTX, None)),
        check_vma=False,
    )
```

```python
import functools
import math

import jax
import jax.numpy as jnp
from jax import lax
from jax.experimental import pallas as pl
from jax.experimental.pallas import tpu as pltpu
from jax.sharding import Mesh, PartitionSpec as P

F32 = jnp.float32
BF16 = jnp.bfloat16
HIGHEST = lax.Precision.HIGHEST
DP = ("x", "h")
CTX = ("y", "z", "c")
SPREAD = ("x", "h", "c")
RIM = 16
LANES = 128
TILE = 8
STEP = 256
PANEL = 16
PARAMS = pltpu.CompilerParams(vmem_limit_bytes=48 << 20)


def conv_kernel(
    place_ref, block_hbm, other_ref, near_ref, far_ref, taps_hbm, act_ref,
    block_ref, taps_ref, wide_ref, sums_ref, weights_ref, sems,
):
    count, frames, width = block_ref.shape
    rows = 2 * frames + 2 * RIM
    core = place_ref[0]
    lane = lax.broadcasted_iota(jnp.int32, (1, LANES), 1)
    first = lax.rem(lane // 16, 2) == place_ref[1]
    own = pl.multiple_of(RIM + frames * core, RIM)
    partner = pl.multiple_of(RIM + frames * (1 - core), RIM)
    pairs = STEP // (2 * TILE)

    def block_copy(index):
        cols = pl.ds(pl.multiple_of(index * width, width), width)
        return pltpu.make_async_copy(block_hbm.at[:, cols], block_ref.at[index], sems.at[index])

    def picked(value):
        value = value.astype(F32)
        return jnp.where(first, value[:, :LANES], value[:, LANES:])

    taps_copy = pltpu.make_async_copy(taps_hbm, taps_ref, sems.at[count])
    for index in range(count):
        block_copy(index).start()
        if index == 0:
            taps_copy.start()

    def group(step, _):
        cols = pl.ds(pl.multiple_of(step * width, width), width)
        out_cols = pl.ds(pl.multiple_of(step * LANES, LANES), LANES)
        near, far = picked(near_ref[:, cols]), picked(far_ref[:, cols])
        wide_ref[0:RIM] = jnp.where(core == 0, near, far)
        wide_ref[rows - RIM : rows] = jnp.where(core == 0, far, near)
        wide_ref[pl.ds(partner, frames)] = picked(other_ref[:, cols])

        @pl.when(step == 0)
        def _():
            taps_copy.wait()

        weights_ref[0:1] = jnp.zeros((1, LANES), F32)
        weights_ref[1:32] = picked(taps_ref[:, cols])
        weights_ref[32:40] = weights_ref[0:8] + weights_ref[8:16]
        weights_ref[40:48] = weights_ref[16:24] + weights_ref[24:32]
        block_copy(step).wait()
        wide_ref[pl.ds(own, frames)] = picked(block_ref[step])
        sums_ref[0 : rows - TILE] = wide_ref[0 : rows - TILE] + wide_ref[TILE:rows]

        def chunk(index, _):
            base = pl.multiple_of(index * STEP, STEP)
            even, odd, both = [None] * (pairs + 1), [None] * pairs, [None] * pairs

            def add(totals, place, weight, value):
                term = weight * value
                totals[place] = term if totals[place] is None else totals[place] + term

            for shift in range(TILE):

                def weight(row):
                    return weights_ref[row + shift : row + shift + 1]

                def tiles(ref, start, number):
                    return [
                        ref[pl.ds(base + shift + TILE * (start + 2 * k), TILE)] for k in range(number)
                    ]

                values = tiles(wide_ref, 0, pairs + 2)
                for k in range(pairs + 1):
                    if shift:
                        add(even, k, weight(0), values[k])
                    add(even, k, weight(16), values[k + 1])
                values = tiles(wide_ref, 1, pairs + 1)
                for k in range(pairs):
                    add(odd, k, weight(8), values[k])
                    add(odd, k, weight(24), values[k + 1])
                values = tiles(sums_ref, 1, pairs + 1)
                for k in range(pairs):
                    add(both, k, weight(32), values[k])
                    add(both, k, weight(40), values[k + 1])
            for k in range(pairs):
                total = jnp.concatenate(
                    [even[k] + odd[k], both[k] - (even[k + 1] + odd[k])], axis=0
                )
                half = 0.5 * total
                place = pl.ds(pl.multiple_of(base + 2 * TILE * k, 2 * TILE), 2 * TILE)
                act_ref[place, out_cols] = (half + half * jnp.tanh(half)).astype(BF16)
            return 0

        lax.fori_loop(0, 2 * frames // STEP, chunk, 0)
        return 0

    lax.fori_loop(0, count, group, 0)


def activation(place, block, other, near, far, taps):
    frames, channels = block.shape
    width = 2 * LANES
    count = channels // width
    rows = 2 * frames + 2 * RIM
    smem, vmem, hbm = (
        pl.BlockSpec(memory_space=space) for space in (pltpu.SMEM, pltpu.VMEM, pltpu.HBM)
    )
    block, taps = (pltpu.with_memory_space_constraint(array, pltpu.HBM) for array in (block, taps))
    return pl.pallas_call(
        conv_kernel,
        in_specs=[smem, hbm, vmem, vmem, vmem, hbm],
        out_specs=vmem,
        out_shape=pltpu.VMEM((2 * frames, channels // 2), BF16),
        scratch_shapes=[
            pltpu.VMEM((count, frames, width), BF16),
            pltpu.VMEM(taps.shape, F32),
            pltpu.VMEM((rows, LANES), F32),
            pltpu.VMEM((rows, LANES), F32),
            pltpu.VMEM((48, LANES), F32),
            pltpu.SemaphoreType.DMA((count + 1,)),
        ],
        compiler_params=PARAMS,
        name="activation",
    )(place, block, other, near, far, taps)


def product_kernel(place_ref, act_ref, own_ref, other_ref, product_ref):
    frames = own_ref.shape[0]
    core = place_ref[0]

    def part(first, signal_ref):
        act = act_ref[pl.ds(pl.multiple_of(first, frames), frames)]
        return lax.dot_general(
            act, signal_ref[...], (((0,), (0,)), ((), ())), preferred_element_type=F32
        )

    total = part(frames * core, own_ref) + part(frames * (1 - core), other_ref)
    blocks, _, quarter, owned, features = product_ref.shape
    pieces = total.reshape(blocks, quarter, 2, owned, features).astype(BF16)
    for parity in range(2):
        product_ref[:, lax.rem(parity + place_ref[1], 2)] = pieces[:, :, parity]


def merge_kernel(inverse_root, parts_ref, carried_ref, right_ref, merged_ref, shares_ref):
    total = parts_ref[0].astype(F32)
    for index in range(1, parts_ref.shape[0]):
        total = total + parts_ref[index].astype(F32)
    merged = total * inverse_root + carried_ref[...]
    merged_ref[...] = merged
    left = lax.dot_general(
        merged, right_ref[...], (((1,), (1,)), ((), ())), precision=HIGHEST, preferred_element_type=F32
    )
    owned = left.shape[0]
    packed = jnp.concatenate([left[: owned // 2], left[owned // 2 :]], axis=1)
    copies = shares_ref.shape[0] * LANES // merged.shape[1]
    for index in range(shares_ref.shape[0]):
        first = LANES * (index // copies)
        shares_ref[index, :owned] = merged[:, first : first + LANES]
        shares_ref[index, owned:] = packed


def term_kernel(place_ref, parts_ref, left_ref, term_ref, rows_ref, gram_ref):
    owned, rank = left_ref.shape
    sources = rows_ref.shape[0]
    lefts, means = [], []
    for source in range(sources):
        total = parts_ref[source]
        for index in range(source + sources, parts_ref.shape[0], sources):
            total = total + parts_ref[index]
        packed = total[owned:]
        left = jnp.concatenate([packed[:, :rank], packed[:, rank:]], axis=0)
        rows_ref[source] = left
        lefts.append(left)
        means.append(total[:owned])
    left_ref[...] = rows_ref[place_ref[3]]
    left, mean = jnp.concatenate(lefts, axis=0), jnp.concatenate(means, axis=0)
    dot = functools.partial(
        lax.dot_general,
        dimension_numbers=(((0,), (0,)), ((), ())),
        precision=HIGHEST,
        preferred_element_type=F32,
    )
    term = dot(left, mean)
    gram_ref[...] = dot(left, jnp.concatenate([jnp.zeros_like(left), left], axis=1))
    gram = gram_ref[pl.ds(pl.multiple_of(TILE * place_ref[2], TILE), TILE)]
    for index in range(term_ref.shape[0]):
        term_ref[index, :rank] = term
        term_ref[index, rank:] = gram


def total_kernel(parts_ref, total_ref):
    total = parts_ref[0]
    for index in range(1, parts_ref.shape[0]):
        total = total + parts_ref[index]
    for index in range(total_ref.shape[0]):
        total_ref[index] = total


def eliminate(rest, rank):
    done = []
    for start in range(0, rank, PANEL):
        row = lax.broadcasted_iota(jnp.int32, rest.shape, 0)
        first = rank + start
        columns = [
            jnp.broadcast_to(rest[:, first + j : first + j + 1], rest.shape) for j in range(PANEL)
        ]
        top = rest[:PANEL]
        scaled = []
        for j in range(PANEL):
            inverse = 1.0 / columns[j][j : j + 1]
            scaled.append(top[j : j + 1] * inverse)
            below = jnp.where(row > j, columns[j], 0.0)
            columns[j] = below
            for i in range(j + 1, PANEL):
                columns[i] = columns[i] - below * (columns[i][j : j + 1] * inverse)
            top = top - below[:PANEL] * scaled[j]
        done.append(top)
        rest = rest[PANEL:]
        if start + PANEL < rank:
            for j in range(PANEL):
                rest = rest - columns[j][PANEL:] * scaled[j]
    return jnp.concatenate(done, axis=0)


def finish_kernel(replicas, rows_ref, left_ref, merged_ref, right_ref, estimate_ref, error_ref, wide_ref):
    rank = left_ref.shape[1]
    features = merged_ref.shape[1]
    for index in range(rows_ref.shape[0]):
        wide_ref[:, LANES * index : LANES * (index + 1)] = rows_ref[index, :rank]
        wide_ref[TILE * index : TILE * (index + 1), features:] = rows_ref[index, rank:]
    row = lax.broadcasted_iota(jnp.int32, (rank, 2 * rank), 0)
    lane = lax.broadcasted_iota(jnp.int32, (rank, 2 * rank), 1)
    work = eliminate(wide_ref[:, features:] + (row == lane).astype(F32), rank)
    pivots = jnp.sum(jnp.where(row + rank == lane, work, 0.0), axis=1, keepdims=True)
    inverse = (work * (1.0 / jnp.sqrt(pivots)))[:, :rank]
    dot = functools.partial(lax.dot_general, precision=HIGHEST, preferred_element_type=F32)
    right = dot(inverse, wide_ref[:, :features], (((1,), (0,)), ((), ()))) * (1.0 / replicas)
    right_ref[...] = right
    left_hat = dot(left_ref[...], inverse, (((1,), (1,)), ((), ())))
    estimate = dot(left_hat, right, (((1,), (0,)), ((), ())))
    estimate_ref[...] = estimate
    error_ref[...] = merged_ref[...] - estimate


def call(kernel, outs, *args, smem=0, scratch=()):
    spaces = [pltpu.SMEM] * smem + [pltpu.VMEM] * (len(args) - smem)
    return pl.pallas_call(
        kernel,
        in_specs=[pl.BlockSpec(memory_space=space) for space in spaces],
        out_shape=[jax.ShapeDtypeStruct(out, F32) if isinstance(out, tuple) else out for out in outs],
        scratch_shapes=list(scratch),
        compiler_params=PARAMS,
        name=getattr(kernel, "func", kernel).__name__,
    )(*args)


def exchange(block, axes, groups=None):
    return lax.all_to_all(block, axes, 0, 0, tiled=True, axis_index_groups=groups)


def local(gated_input, upstream, depth_kernel, carried_error, right_init):
    replicas = lax.axis_size(DP)
    contexts = lax.axis_size(CTX)
    block = gated_input[0]
    frames, channels = block.shape
    features = upstream.shape[2]
    rank = right_init.shape[1]
    owned = channels // contexts
    core = lax.axis_index("c")
    swap = [(0, 1), (1, 0)]
    ends = lax.dynamic_slice_in_dim(block, core * (frames - RIM), RIM, axis=0)
    one = [(i, i + 1 if i % 2 else i - 1) for i in range(1, contexts - 1)]
    two = [(i, i + 2 if i % 2 else i - 2) for i in range(1, contexts - 1)]
    ends, block = lax.optimization_barrier((ends, block))
    near = lax.ppermute(ends, CTX, one)
    far = lax.ppermute(ends, CTX, two)
    other = lax.ppermute(block, "c", swap)
    signal = upstream[0]
    other_signal = lax.ppermute(signal, "c", swap)
    depth = lax.axis_size("z")
    side = [(2 * z) // depth for z in range(depth)]
    teams = [
        [2 * chip + (team + side[chip % depth]) % 2 for chip in range(contexts // 2)]
        for team in range(2)
    ]
    team = lax.rem(core + (2 * lax.axis_index("z")) // depth, 2)
    place = jnp.stack([core, team, lax.axis_index(DP), lax.axis_index("c")])
    act = activation(place, block, other, near, far, depth_kernel)
    (product,) = call(
        product_kernel,
        [pltpu.VMEM((channels // 256, 2, 4, owned, features), BF16)],
        place,
        act,
        signal,
        other_signal,
        smem=1,
    )
    inverse_root = 1.0 / math.sqrt(frames * contexts)
    row = (owned, features)
    spread = lax.axis_size(SPREAD)
    merged, shares = call(
        functools.partial(merge_kernel, inverse_root),
        [row, pltpu.VMEM((spread, owned + owned // 2, LANES), F32)],
        exchange(product.reshape(channels // 32, owned, features), CTX, teams),
        carried_error[0],
        right_init.T,
    )
    size = (rank + TILE, LANES)
    left, term = call(
        term_kernel,
        [(owned, rank), pltpu.VMEM((lax.axis_size("y"), *size), F32)],
        place,
        exchange(shares, SPREAD),
        smem=1,
        scratch=[pltpu.VMEM((spread // replicas, owned, rank), F32), pltpu.VMEM((rank, LANES), F32)],
    )
    (total,) = call(total_kernel, [pltpu.VMEM((lax.axis_size("z"), *size), F32)], exchange(term, "y"))
    (total,) = call(total_kernel, [pltpu.VMEM((replicas, *size), F32)], exchange(total, "z"))
    right, estimate, error = call(
        functools.partial(finish_kernel, replicas),
        [(rank, features), row, row],
        exchange(total, DP),
        left,
        merged,
        scratch=[pltpu.VMEM((rank, features + 2 * rank), F32)],
    )
    return right.T, estimate, error[None]


def solution(mesh):
    wide = Mesh(mesh.devices.reshape(4, 2, 4, 8, 2), ("x", "h", "y", "z", "c"))
    return jax.shard_map(
        local,
        mesh=wide,
        in_specs=(P(DP, CTX, None), P(DP, CTX, None), P(), P(DP, CTX, None), P()),
        out_specs=(P(), P(CTX, None), P(DP, CTX, None)),
        check_vma=False,
    )
```

```python
import functools
import math

import jax
import jax.numpy as jnp
from jax import lax
from jax.experimental import pallas as pl
from jax.experimental.pallas import tpu as pltpu
from jax.sharding import Mesh, PartitionSpec as P

F32 = jnp.float32
BF16 = jnp.bfloat16
HIGHEST = lax.Precision.HIGHEST
DP = ("x", "h")
CTX = ("y", "z", "c")
SPREAD = ("x", "h", "c")
RIM = 16
LANES = 128
TILE = 8
STEP = 256
PANEL = 16
PARAMS = pltpu.CompilerParams(vmem_limit_bytes=48 << 20)


def conv_kernel(
    place_ref, block_hbm, other_ref, near_ref, far_ref, taps_hbm, act_ref,
    block_ref, taps_ref, wide_ref, sums_ref, weights_ref, sems,
):
    count, frames, width = block_ref.shape
    rows = 2 * frames + 2 * RIM
    core = place_ref[0]
    lane = lax.broadcasted_iota(jnp.int32, (1, LANES), 1)
    first = lax.rem(lane // 16, 2) == place_ref[1]
    own = pl.multiple_of(RIM + frames * core, RIM)
    partner = pl.multiple_of(RIM + frames * (1 - core), RIM)
    pairs = STEP // (2 * TILE)

    def block_copy(index):
        cols = pl.ds(pl.multiple_of(index * width, width), width)
        return pltpu.make_async_copy(block_hbm.at[:, cols], block_ref.at[index], sems.at[index])

    def picked(value):
        value = value.astype(F32)
        return jnp.where(first, value[:, :LANES], value[:, LANES:])

    taps_copy = pltpu.make_async_copy(taps_hbm, taps_ref, sems.at[count])
    for index in range(count):
        block_copy(index).start()
        if index == 0:
            taps_copy.start()

    def group(step, _):
        cols = pl.ds(pl.multiple_of(step * width, width), width)
        out_cols = pl.ds(pl.multiple_of(step * LANES, LANES), LANES)
        near, far = picked(near_ref[:, cols]), picked(far_ref[:, cols])
        wide_ref[0:RIM] = jnp.where(core == 0, near, far)
        wide_ref[rows - RIM : rows] = jnp.where(core == 0, far, near)
        wide_ref[pl.ds(partner, frames)] = picked(other_ref[:, cols])

        @pl.when(step == 0)
        def _():
            taps_copy.wait()

        weights_ref[0:1] = jnp.zeros((1, LANES), F32)
        weights_ref[1:32] = picked(taps_ref[:, cols])
        weights_ref[32:40] = weights_ref[0:8] + weights_ref[8:16]
        weights_ref[40:48] = weights_ref[16:24] + weights_ref[24:32]
        block_copy(step).wait()
        wide_ref[pl.ds(own, frames)] = picked(block_ref[step])
        sums_ref[0 : rows - TILE] = wide_ref[0 : rows - TILE] + wide_ref[TILE:rows]

        def chunk(index, _):
            base = pl.multiple_of(index * STEP, STEP)
            even, odd, both = [None] * (pairs + 1), [None] * pairs, [None] * pairs

            def add(totals, place, weight, value):
                term = weight * value
                totals[place] = term if totals[place] is None else totals[place] + term

            for shift in range(TILE):

                def weight(row):
                    return weights_ref[row + shift : row + shift + 1]

                def tiles(ref, start, number):
                    return [
                        ref[pl.ds(base + shift + TILE * (start + 2 * k), TILE)] for k in range(number)
                    ]

                values = tiles(wide_ref, 0, pairs + 2)
                for k in range(pairs + 1):
                    if shift:
                        add(even, k, weight(0), values[k])
                    add(even, k, weight(16), values[k + 1])
                values = tiles(wide_ref, 1, pairs + 1)
                for k in range(pairs):
                    add(odd, k, weight(8), values[k])
                    add(odd, k, weight(24), values[k + 1])
                values = tiles(sums_ref, 1, pairs + 1)
                for k in range(pairs):
                    add(both, k, weight(32), values[k])
                    add(both, k, weight(40), values[k + 1])
            for k in range(pairs):
                total = jnp.concatenate(
                    [even[k] + odd[k], both[k] - (even[k + 1] + odd[k])], axis=0
                )
                half = 0.5 * total
                place = pl.ds(pl.multiple_of(base + 2 * TILE * k, 2 * TILE), 2 * TILE)
                act_ref[place, out_cols] = (half + half * jnp.tanh(half)).astype(BF16)
            return 0

        lax.fori_loop(0, 2 * frames // STEP, chunk, 0)
        return 0

    lax.fori_loop(0, count, group, 0)


def activation(place, block, other, near, far, taps):
    frames, channels = block.shape
    width = 2 * LANES
    count = channels // width
    rows = 2 * frames + 2 * RIM
    smem, vmem, hbm = (
        pl.BlockSpec(memory_space=space) for space in (pltpu.SMEM, pltpu.VMEM, pltpu.HBM)
    )
    block, taps = (pltpu.with_memory_space_constraint(array, pltpu.HBM) for array in (block, taps))
    return pl.pallas_call(
        conv_kernel,
        in_specs=[smem, hbm, vmem, vmem, vmem, hbm],
        out_specs=vmem,
        out_shape=pltpu.VMEM((2 * frames, channels // 2), BF16),
        scratch_shapes=[
            pltpu.VMEM((count, frames, width), BF16),
            pltpu.VMEM(taps.shape, F32),
            pltpu.VMEM((rows, LANES), F32),
            pltpu.VMEM((rows, LANES), F32),
            pltpu.VMEM((48, LANES), F32),
            pltpu.SemaphoreType.DMA((count + 1,)),
        ],
        compiler_params=PARAMS,
        name="activation",
    )(place, block, other, near, far, taps)


def product_kernel(place_ref, act_ref, own_ref, other_ref, product_ref):
    frames = own_ref.shape[0]
    core = place_ref[0]

    def part(first, signal_ref):
        act = act_ref[pl.ds(pl.multiple_of(first, frames), frames)]
        return lax.dot_general(
            act, signal_ref[...], (((0,), (0,)), ((), ())), preferred_element_type=F32
        )

    total = part(frames * core, own_ref) + part(frames * (1 - core), other_ref)
    blocks, _, quarter, owned, features = product_ref.shape
    pieces = total.reshape(blocks, quarter, 2, owned, features).astype(BF16)
    for parity in range(2):
        product_ref[:, lax.rem(parity + place_ref[1], 2)] = pieces[:, :, parity]


def merge_kernel(inverse_root, parts_ref, carried_ref, right_ref, merged_ref, shares_ref):
    total = parts_ref[0].astype(F32)
    for index in range(1, parts_ref.shape[0]):
        total = total + parts_ref[index].astype(F32)
    merged = total * inverse_root + carried_ref[...]
    merged_ref[...] = merged
    left = lax.dot_general(
        merged, right_ref[...], (((1,), (1,)), ((), ())), precision=HIGHEST, preferred_element_type=F32
    )
    owned = left.shape[0]
    packed = jnp.concatenate([left[: owned // 2], left[owned // 2 :]], axis=1)
    copies = shares_ref.shape[0] * LANES // merged.shape[1]
    for index in range(shares_ref.shape[0]):
        first = LANES * (index // copies)
        shares_ref[index, :owned] = merged[:, first : first + LANES]
        shares_ref[index, owned:] = packed


def term_kernel(place_ref, parts_ref, left_ref, term_ref, rows_ref, gram_ref):
    owned, rank = left_ref.shape
    sources = rows_ref.shape[0]
    lefts, means = [], []
    for source in range(sources):
        total = parts_ref[source]
        for index in range(source + sources, parts_ref.shape[0], sources):
            total = total + parts_ref[index]
        packed = total[owned:]
        left = jnp.concatenate([packed[:, :rank], packed[:, rank:]], axis=0)
        rows_ref[source] = left
        lefts.append(left)
        means.append(total[:owned])
    left_ref[...] = rows_ref[place_ref[3]]
    left, mean = jnp.concatenate(lefts, axis=0), jnp.concatenate(means, axis=0)
    dot = functools.partial(
        lax.dot_general,
        dimension_numbers=(((0,), (0,)), ((), ())),
        precision=HIGHEST,
        preferred_element_type=F32,
    )
    both = dot(left, jnp.concatenate([mean, jnp.zeros_like(left), left], axis=1))
    term = both[:, :LANES]
    gram_ref[...] = both[:, LANES:]
    gram = gram_ref[pl.ds(pl.multiple_of(TILE * place_ref[2], TILE), TILE)]
    gram_ref[...] = term
    term = gram_ref[pl.ds(pl.multiple_of(rank // 2 * place_ref[3], rank // 2), rank // 2)]
    for index in range(term_ref.shape[0]):
        term_ref[index, : rank // 2] = term
        term_ref[index, rank // 2 :] = gram


def total_kernel(parts_ref, total_ref):
    total = parts_ref[0]
    for index in range(1, parts_ref.shape[0]):
        total = total + parts_ref[index]
    for index in range(total_ref.shape[0]):
        total_ref[index] = total


def eliminate(rest, rank):
    done = []
    for start in range(0, rank, PANEL):
        row = lax.broadcasted_iota(jnp.int32, rest.shape, 0)
        first = rank + start
        columns = [
            jnp.broadcast_to(rest[:, first + j : first + j + 1], rest.shape) for j in range(PANEL)
        ]
        top = rest[:PANEL]
        scaled = []
        for j in range(PANEL):
            inverse = 1.0 / columns[j][j : j + 1]
            scaled.append(top[j : j + 1] * inverse)
            below = jnp.where(row > j, columns[j], 0.0)
            columns[j] = below
            for i in range(j + 1, PANEL):
                columns[i] = columns[i] - below * (columns[i][j : j + 1] * inverse)
            top = top - below[:PANEL] * scaled[j]
        done.append(top)
        rest = rest[PANEL:]
        if start + PANEL < rank:
            for j in range(PANEL):
                rest = rest - columns[j][PANEL:] * scaled[j]
    return jnp.concatenate(done, axis=0)


def finish_kernel(replicas, rows_ref, left_ref, merged_ref, right_ref, estimate_ref, error_ref, wide_ref):
    rank = left_ref.shape[1]
    features = merged_ref.shape[1]
    half = rank // 2
    for index in range(rows_ref.shape[1]):
        cols = slice(LANES * index, LANES * (index + 1))
        wide_ref[:half, cols] = rows_ref[0, index, :half]
        wide_ref[half:, cols] = rows_ref[1, index, :half]
        wide_ref[TILE * index : TILE * (index + 1), features:] = rows_ref[0, index, half:]
    row = lax.broadcasted_iota(jnp.int32, (rank, 2 * rank), 0)
    lane = lax.broadcasted_iota(jnp.int32, (rank, 2 * rank), 1)
    work = eliminate(wide_ref[:, features:] + (row == lane).astype(F32), rank)
    pivots = jnp.sum(jnp.where(row + rank == lane, work, 0.0), axis=1, keepdims=True)
    inverse = (work * (1.0 / jnp.sqrt(pivots)))[:, :rank]
    dot = functools.partial(lax.dot_general, precision=HIGHEST, preferred_element_type=F32)
    right = dot(inverse, wide_ref[:, :features], (((1,), (0,)), ((), ()))) * (1.0 / replicas)
    right_ref[...] = right
    left_hat = dot(left_ref[...], inverse, (((1,), (1,)), ((), ())))
    estimate = dot(left_hat, right, (((1,), (0,)), ((), ())))
    estimate_ref[...] = estimate
    error_ref[...] = merged_ref[...] - estimate


def call(kernel, outs, *args, smem=0, scratch=()):
    spaces = [pltpu.SMEM] * smem + [pltpu.VMEM] * (len(args) - smem)
    return pl.pallas_call(
        kernel,
        in_specs=[pl.BlockSpec(memory_space=space) for space in spaces],
        out_shape=[jax.ShapeDtypeStruct(out, F32) if isinstance(out, tuple) else out for out in outs],
        scratch_shapes=list(scratch),
        compiler_params=PARAMS,
        name=getattr(kernel, "func", kernel).__name__,
    )(*args)


def exchange(block, axes, groups=None):
    return lax.all_to_all(block, axes, 0, 0, tiled=True, axis_index_groups=groups)


def local(gated_input, upstream, depth_kernel, carried_error, right_init):
    replicas = lax.axis_size(DP)
    contexts = lax.axis_size(CTX)
    block = gated_input[0]
    frames, channels = block.shape
    features = upstream.shape[2]
    rank = right_init.shape[1]
    owned = channels // contexts
    core = lax.axis_index("c")
    swap = [(0, 1), (1, 0)]
    ends = lax.dynamic_slice_in_dim(block, core * (frames - RIM), RIM, axis=0)
    one = [(i, i + 1 if i % 2 else i - 1) for i in range(1, contexts - 1)]
    two = [(i, i + 2 if i % 2 else i - 2) for i in range(1, contexts - 1)]
    ends, block = lax.optimization_barrier((ends, block))
    near = lax.ppermute(ends, CTX, one)
    far = lax.ppermute(ends, CTX, two)
    other = lax.ppermute(block, "c", swap)
    signal = upstream[0]
    other_signal = lax.ppermute(signal, "c", swap)
    depth = lax.axis_size("z")
    side = [(2 * z) // depth for z in range(depth)]
    teams = [
        [2 * chip + (team + side[chip % depth]) % 2 for chip in range(contexts // 2)]
        for team in range(2)
    ]
    team = lax.rem(core + (2 * lax.axis_index("z")) // depth, 2)
    place = jnp.stack([core, team, lax.axis_index(DP), lax.axis_index("c")])
    act = activation(place, block, other, near, far, depth_kernel)
    (product,) = call(
        product_kernel,
        [pltpu.VMEM((channels // 256, 2, 4, owned, features), BF16)],
        place,
        act,
        signal,
        other_signal,
        smem=1,
    )
    inverse_root = 1.0 / math.sqrt(frames * contexts)
    row = (owned, features)
    spread = lax.axis_size(SPREAD)
    merged, shares = call(
        functools.partial(merge_kernel, inverse_root),
        [row, pltpu.VMEM((spread, owned + owned // 2, LANES), F32)],
        exchange(product.reshape(channels // 32, owned, features), CTX, teams),
        carried_error[0],
        right_init.T,
    )
    size = (rank // 2 + TILE, LANES)
    left, term = call(
        term_kernel,
        [(owned, rank), pltpu.VMEM((lax.axis_size("y"), *size), F32)],
        place,
        exchange(shares, SPREAD),
        smem=1,
        scratch=[pltpu.VMEM((spread // replicas, owned, rank), F32), pltpu.VMEM((rank, LANES), F32)],
    )
    (total,) = call(total_kernel, [pltpu.VMEM((lax.axis_size("z"), *size), F32)], exchange(term, "y"))
    (total,) = call(total_kernel, [pltpu.VMEM((replicas, *size), F32)], exchange(total, "z"))
    right, estimate, error = call(
        functools.partial(finish_kernel, replicas),
        [(rank, features), row, row],
        lax.all_gather(exchange(total, DP), "c"),
        left,
        merged,
        scratch=[pltpu.VMEM((rank, features + 2 * rank), F32)],
    )
    return right.T, estimate, error[None]


def solution(mesh):
    wide = Mesh(mesh.devices.reshape(4, 2, 4, 8, 2), ("x", "h", "y", "z", "c"))
    return jax.shard_map(
        local,
        mesh=wide,
        in_specs=(P(DP, CTX, None), P(DP, CTX, None), P(), P(DP, CTX, None), P()),
        out_specs=(P(), P(CTX, None), P(DP, CTX, None)),
        check_vma=False,
    )
```

```python
import functools
import math

import jax
import jax.numpy as jnp
from jax import lax
from jax.experimental import pallas as pl
from jax.experimental.pallas import tpu as pltpu
from jax.sharding import Mesh, PartitionSpec as P

F32 = jnp.float32
BF16 = jnp.bfloat16
HIGHEST = lax.Precision.HIGHEST
DP = ("x", "h")
CTX = ("y", "z", "c")
SPREAD = ("x", "h", "c")
RIM = 16
LANES = 128
TILE = 8
STEP = 256
PANEL = 16
PARAMS = pltpu.CompilerParams(vmem_limit_bytes=48 << 20)


def conv_kernel(
    place_ref, block_hbm, other_ref, near_ref, far_ref, taps_hbm, act_ref,
    block_ref, taps_ref, wide_ref, sums_ref, weights_ref, sems,
):
    count, frames, width = block_ref.shape
    rows = 2 * frames + 2 * RIM
    core = place_ref[0]
    lane = lax.broadcasted_iota(jnp.int32, (1, LANES), 1)
    first = lax.rem(lane // 16, 2) == place_ref[1]
    own = pl.multiple_of(RIM + frames * core, RIM)
    partner = pl.multiple_of(RIM + frames * (1 - core), RIM)
    pairs = STEP // (2 * TILE)

    def block_copy(index):
        cols = pl.ds(pl.multiple_of(index * width, width), width)
        return pltpu.make_async_copy(block_hbm.at[:, cols], block_ref.at[index], sems.at[index])

    def picked(value):
        value = value.astype(F32)
        return jnp.where(first, value[:, :LANES], value[:, LANES:])

    taps_copy = pltpu.make_async_copy(taps_hbm, taps_ref, sems.at[count])
    for index in range(count):
        block_copy(index).start()
        if index == 0:
            taps_copy.start()

    def group(step, _):
        cols = pl.ds(pl.multiple_of(step * width, width), width)
        out_cols = pl.ds(pl.multiple_of(step * LANES, LANES), LANES)
        near, far = picked(near_ref[:, cols]), picked(far_ref[:, cols])
        wide_ref[0:RIM] = jnp.where(core == 0, near, far)
        wide_ref[rows - RIM : rows] = jnp.where(core == 0, far, near)
        wide_ref[pl.ds(partner, frames)] = picked(other_ref[:, cols])

        @pl.when(step == 0)
        def _():
            taps_copy.wait()

        weights_ref[0:1] = jnp.zeros((1, LANES), F32)
        weights_ref[1:32] = picked(taps_ref[:, cols])
        weights_ref[32:40] = weights_ref[0:8] + weights_ref[8:16]
        weights_ref[40:48] = weights_ref[16:24] + weights_ref[24:32]
        block_copy(step).wait()
        wide_ref[pl.ds(own, frames)] = picked(block_ref[step])
        sums_ref[0 : rows - TILE] = wide_ref[0 : rows - TILE] + wide_ref[TILE:rows]

        def chunk(index, _):
            base = pl.multiple_of(index * STEP, STEP)
            even, odd, both = [None] * (pairs + 1), [None] * pairs, [None] * pairs

            def add(totals, place, weight, value):
                term = weight * value
                totals[place] = term if totals[place] is None else totals[place] + term

            for shift in range(TILE):

                def weight(row):
                    return weights_ref[row + shift : row + shift + 1]

                def tiles(ref, start, number):
                    return [
                        ref[pl.ds(base + shift + TILE * (start + 2 * k), TILE)] for k in range(number)
                    ]

                values = tiles(wide_ref, 0, pairs + 2)
                for k in range(pairs + 1):
                    if shift:
                        add(even, k, weight(0), values[k])
                    add(even, k, weight(16), values[k + 1])
                values = tiles(wide_ref, 1, pairs + 1)
                for k in range(pairs):
                    add(odd, k, weight(8), values[k])
                    add(odd, k, weight(24), values[k + 1])
                values = tiles(sums_ref, 1, pairs + 1)
                for k in range(pairs):
                    add(both, k, weight(32), values[k])
                    add(both, k, weight(40), values[k + 1])
            for k in range(pairs):
                total = jnp.concatenate(
                    [even[k] + odd[k], both[k] - (even[k + 1] + odd[k])], axis=0
                )
                half = 0.5 * total
                place = pl.ds(pl.multiple_of(base + 2 * TILE * k, 2 * TILE), 2 * TILE)
                act_ref[place, out_cols] = (half + half * jnp.tanh(half)).astype(BF16)
            return 0

        lax.fori_loop(0, 2 * frames // STEP, chunk, 0)
        return 0

    lax.fori_loop(0, count, group, 0)


def activation(place, block, other, near, far, taps):
    frames, channels = block.shape
    width = 2 * LANES
    count = channels // width
    rows = 2 * frames + 2 * RIM
    smem, vmem, hbm = (
        pl.BlockSpec(memory_space=space) for space in (pltpu.SMEM, pltpu.VMEM, pltpu.HBM)
    )
    block, taps = (pltpu.with_memory_space_constraint(array, pltpu.HBM) for array in (block, taps))
    return pl.pallas_call(
        conv_kernel,
        in_specs=[smem, hbm, vmem, vmem, vmem, hbm],
        out_specs=vmem,
        out_shape=pltpu.VMEM((2 * frames, channels // 2), BF16),
        scratch_shapes=[
            pltpu.VMEM((count, frames, width), BF16),
            pltpu.VMEM(taps.shape, F32),
            pltpu.VMEM((rows, LANES), F32),
            pltpu.VMEM((rows, LANES), F32),
            pltpu.VMEM((48, LANES), F32),
            pltpu.SemaphoreType.DMA((count + 1,)),
        ],
        compiler_params=PARAMS,
        name="activation",
    )(place, block, other, near, far, taps)


def product_kernel(place_ref, act_ref, own_ref, other_ref, product_ref):
    frames = own_ref.shape[0]
    core = place_ref[0]

    def part(first, signal_ref):
        act = act_ref[pl.ds(pl.multiple_of(first, frames), frames)]
        return lax.dot_general(
            act, signal_ref[...], (((0,), (0,)), ((), ())), preferred_element_type=F32
        )

    total = part(frames * core, own_ref) + part(frames * (1 - core), other_ref)
    blocks, _, quarter, owned, features = product_ref.shape
    pieces = total.reshape(blocks, quarter, 2, owned, features).astype(BF16)
    for parity in range(2):
        product_ref[:, lax.rem(parity + place_ref[1], 2)] = pieces[:, :, parity]


def merge_kernel(inverse_root, parts_ref, carried_ref, right_ref, merged_ref, shares_ref):
    total = parts_ref[0].astype(F32)
    for index in range(1, parts_ref.shape[0]):
        total = total + parts_ref[index].astype(F32)
    merged = total * inverse_root + carried_ref[...]
    merged_ref[...] = merged
    left = lax.dot_general(
        merged, right_ref[...], (((1,), (1,)), ((), ())), precision=HIGHEST, preferred_element_type=F32
    )
    owned = left.shape[0]
    packed = jnp.concatenate([left[: owned // 2], left[owned // 2 :]], axis=1)
    copies = shares_ref.shape[0] * LANES // merged.shape[1]
    for index in range(shares_ref.shape[0]):
        first = LANES * (index // copies)
        shares_ref[index, :owned] = merged[:, first : first + LANES]
        shares_ref[index, owned:] = packed


def term_kernel(place_ref, parts_ref, left_ref, term_ref, rows_ref, gram_ref):
    owned, rank = left_ref.shape
    sources = rows_ref.shape[0]
    lefts, means = [], []
    for source in range(sources):
        total = parts_ref[source]
        for index in range(source + sources, parts_ref.shape[0], sources):
            total = total + parts_ref[index]
        packed = total[owned:]
        left = jnp.concatenate([packed[:, :rank], packed[:, rank:]], axis=0)
        rows_ref[source] = left
        lefts.append(left)
        means.append(total[:owned])
    left_ref[...] = rows_ref[place_ref[3]]
    left, mean = jnp.concatenate(lefts, axis=0), jnp.concatenate(means, axis=0)
    dot = functools.partial(
        lax.dot_general,
        dimension_numbers=(((0,), (0,)), ((), ())),
        precision=HIGHEST,
        preferred_element_type=F32,
    )
    both = dot(left, jnp.concatenate([mean, jnp.zeros_like(left), left], axis=1))
    term = both[:, :LANES]
    gram_ref[...] = both[:, LANES:]
    gram = gram_ref[pl.ds(pl.multiple_of(TILE * place_ref[2], TILE), TILE)]
    gram_ref[...] = term
    term = gram_ref[pl.ds(pl.multiple_of(rank // 2 * place_ref[3], rank // 2), rank // 2)]
    for index in range(term_ref.shape[0]):
        term_ref[index, : rank // 2] = term
        term_ref[index, rank // 2 :] = gram


def total_kernel(parts_ref, total_ref):
    total = parts_ref[0]
    for index in range(1, parts_ref.shape[0]):
        total = total + parts_ref[index]
    for index in range(total_ref.shape[0]):
        total_ref[index] = total


def eliminate(rest, rank):
    done = []
    for start in range(0, rank, PANEL):
        row = lax.broadcasted_iota(jnp.int32, rest.shape, 0)
        first = rank + start
        columns = [
            jnp.broadcast_to(rest[:, first + j : first + j + 1], rest.shape) for j in range(PANEL)
        ]
        top = rest[:PANEL]
        scaled = []
        for j in range(PANEL):
            inverse = 1.0 / columns[j][j : j + 1]
            scaled.append(top[j : j + 1] * inverse)
            below = jnp.where(row > j, columns[j], 0.0)
            columns[j] = below
            for i in range(j + 1, PANEL):
                columns[i] = columns[i] - below * (columns[i][j : j + 1] * inverse)
            top = top - below[:PANEL] * scaled[j]
        done.append(top)
        rest = rest[PANEL:]
        if start + PANEL < rank:
            for j in range(PANEL):
                rest = rest - columns[j][PANEL:] * scaled[j]
    return jnp.concatenate(done, axis=0)


def finish_kernel(replicas, rows_ref, left_ref, merged_ref, right_ref, estimate_ref, error_ref, wide_ref):
    rank = left_ref.shape[1]
    features = merged_ref.shape[1]
    half = rank // 2
    for index in range(rows_ref.shape[0] // 2):
        cols = slice(LANES * index, LANES * (index + 1))
        wide_ref[:half, cols] = rows_ref[2 * index, :half]
        wide_ref[half:, cols] = rows_ref[2 * index + 1, :half]
        wide_ref[TILE * index : TILE * (index + 1), features:] = rows_ref[2 * index, half:]
    row = lax.broadcasted_iota(jnp.int32, (rank, 2 * rank), 0)
    lane = lax.broadcasted_iota(jnp.int32, (rank, 2 * rank), 1)
    work = eliminate(wide_ref[:, features:] + (row == lane).astype(F32), rank)
    pivots = jnp.sum(jnp.where(row + rank == lane, work, 0.0), axis=1, keepdims=True)
    inverse = (work * (1.0 / jnp.sqrt(pivots)))[:, :rank]
    dot = functools.partial(lax.dot_general, precision=HIGHEST, preferred_element_type=F32)
    right = dot(inverse, wide_ref[:, :features], (((1,), (0,)), ((), ()))) * (1.0 / replicas)
    right_ref[...] = right
    left_hat = dot(left_ref[...], inverse, (((1,), (1,)), ((), ())))
    estimate = dot(left_hat, right, (((1,), (0,)), ((), ())))
    estimate_ref[...] = estimate
    error_ref[...] = merged_ref[...] - estimate


def call(kernel, outs, *args, smem=0, scratch=()):
    spaces = [pltpu.SMEM] * smem + [pltpu.VMEM] * (len(args) - smem)
    return pl.pallas_call(
        kernel,
        in_specs=[pl.BlockSpec(memory_space=space) for space in spaces],
        out_shape=[jax.ShapeDtypeStruct(out, F32) if isinstance(out, tuple) else out for out in outs],
        scratch_shapes=list(scratch),
        compiler_params=PARAMS,
        name=getattr(kernel, "func", kernel).__name__,
    )(*args)


def exchange(block, axes, groups=None):
    return lax.all_to_all(block, axes, 0, 0, tiled=True, axis_index_groups=groups)


def local(gated_input, upstream, depth_kernel, carried_error, right_init):
    replicas = lax.axis_size(DP)
    contexts = lax.axis_size(CTX)
    block = gated_input[0]
    frames, channels = block.shape
    features = upstream.shape[2]
    rank = right_init.shape[1]
    owned = channels // contexts
    core = lax.axis_index("c")
    swap = [(0, 1), (1, 0)]
    ends = lax.dynamic_slice_in_dim(block, core * (frames - RIM), RIM, axis=0)
    one = [(i, i + 1 if i % 2 else i - 1) for i in range(1, contexts - 1)]
    two = [(i, i + 2 if i % 2 else i - 2) for i in range(1, contexts - 1)]
    ends, block = lax.optimization_barrier((ends, block))
    near = lax.ppermute(ends, CTX, one)
    far = lax.ppermute(ends, CTX, two)
    other = lax.ppermute(block, "c", swap)
    signal = upstream[0]
    other_signal = lax.ppermute(signal, "c", swap)
    depth = lax.axis_size("z")
    side = [(2 * z) // depth for z in range(depth)]
    teams = [
        [2 * chip + (team + side[chip % depth]) % 2 for chip in range(contexts // 2)]
        for team in range(2)
    ]
    team = lax.rem(core + (2 * lax.axis_index("z")) // depth, 2)
    place = jnp.stack([core, team, lax.axis_index(DP), lax.axis_index("c")])
    act = activation(place, block, other, near, far, depth_kernel)
    (product,) = call(
        product_kernel,
        [pltpu.VMEM((channels // 256, 2, 4, owned, features), BF16)],
        place,
        act,
        signal,
        other_signal,
        smem=1,
    )
    inverse_root = 1.0 / math.sqrt(frames * contexts)
    row = (owned, features)
    spread = lax.axis_size(SPREAD)
    merged, shares = call(
        functools.partial(merge_kernel, inverse_root),
        [row, pltpu.VMEM((spread, owned + owned // 2, LANES), F32)],
        exchange(product.reshape(channels // 32, owned, features), CTX, teams),
        carried_error[0],
        right_init.T,
    )
    size = (rank // 2 + TILE, LANES)
    left, term = call(
        term_kernel,
        [(owned, rank), pltpu.VMEM((lax.axis_size("y"), *size), F32)],
        place,
        exchange(shares, SPREAD),
        smem=1,
        scratch=[pltpu.VMEM((spread // replicas, owned, rank), F32), pltpu.VMEM((rank, LANES), F32)],
    )
    (total,) = call(total_kernel, [pltpu.VMEM((lax.axis_size("z"), *size), F32)], exchange(term, "y"))
    (total,) = call(total_kernel, [pltpu.VMEM((spread, *size), F32)], exchange(total, "z"))
    right, estimate, error = call(
        functools.partial(finish_kernel, replicas),
        [(rank, features), row, row],
        exchange(total, SPREAD),
        left,
        merged,
        scratch=[pltpu.VMEM((rank, features + 2 * rank), F32)],
    )
    return right.T, estimate, error[None]


def solution(mesh):
    wide = Mesh(mesh.devices.reshape(4, 2, 4, 8, 2), ("x", "h", "y", "z", "c"))
    return jax.shard_map(
        local,
        mesh=wide,
        in_specs=(P(DP, CTX, None), P(DP, CTX, None), P(), P(DP, CTX, None), P()),
        out_specs=(P(), P(CTX, None), P(DP, CTX, None)),
        check_vma=False,
    )
```

```python
import functools
import math

import jax
import jax.numpy as jnp
from jax import lax
from jax.experimental import pallas as pl
from jax.experimental.pallas import tpu as pltpu
from jax.sharding import Mesh, PartitionSpec as P

F32 = jnp.float32
BF16 = jnp.bfloat16
HIGHEST = lax.Precision.HIGHEST
DP = ("x", "h")
CTX = ("y", "z", "c")
SPREAD = ("x", "h", "c")
RIM = 16
LANES = 128
TILE = 8
STEP = 256
PANEL = 16
PARAMS = pltpu.CompilerParams(vmem_limit_bytes=48 << 20)


def conv_kernel(
    place_ref, block_hbm, other_ref, near_ref, far_ref, taps_hbm, act_ref,
    block_ref, taps_ref, wide_ref, sums_ref, weights_ref, sems,
):
    count, frames, width = block_ref.shape
    rows = 2 * frames + 2 * RIM
    core = place_ref[0]
    lane = lax.broadcasted_iota(jnp.int32, (1, LANES), 1)
    first = lax.rem(lane // 16, 2) == place_ref[1]
    own = pl.multiple_of(RIM + frames * core, RIM)
    partner = pl.multiple_of(RIM + frames * (1 - core), RIM)
    pairs = STEP // (2 * TILE)

    def block_copy(index):
        cols = pl.ds(pl.multiple_of(index * width, width), width)
        return pltpu.make_async_copy(block_hbm.at[:, cols], block_ref.at[index], sems.at[index])

    def picked(value):
        value = value.astype(F32)
        return jnp.where(first, value[:, :LANES], value[:, LANES:])

    taps_copy = pltpu.make_async_copy(taps_hbm, taps_ref, sems.at[count])
    for index in range(count):
        block_copy(index).start()
        if index == 0:
            taps_copy.start()

    def group(step, _):
        cols = pl.ds(pl.multiple_of(step * width, width), width)
        out_cols = pl.ds(pl.multiple_of(step * LANES, LANES), LANES)
        near, far = picked(near_ref[:, cols]), picked(far_ref[:, cols])
        wide_ref[0:RIM] = jnp.where(core == 0, near, far)
        wide_ref[rows - RIM : rows] = jnp.where(core == 0, far, near)
        wide_ref[pl.ds(partner, frames)] = picked(other_ref[:, cols])

        @pl.when(step == 0)
        def _():
            taps_copy.wait()

        weights_ref[0:1] = jnp.zeros((1, LANES), F32)
        weights_ref[1:32] = picked(taps_ref[:, cols])
        weights_ref[32:40] = weights_ref[0:8] + weights_ref[8:16]
        weights_ref[40:48] = weights_ref[16:24] + weights_ref[24:32]
        block_copy(step).wait()
        wide_ref[pl.ds(own, frames)] = picked(block_ref[step])
        sums_ref[0 : rows - TILE] = wide_ref[0 : rows - TILE] + wide_ref[TILE:rows]

        def chunk(index, _):
            base = pl.multiple_of(index * STEP, STEP)
            even, odd, both = [None] * (pairs + 1), [None] * pairs, [None] * pairs

            def add(totals, place, weight, value):
                term = weight * value
                totals[place] = term if totals[place] is None else totals[place] + term

            for shift in range(TILE):

                def weight(row):
                    return weights_ref[row + shift : row + shift + 1]

                def tiles(ref, start, number):
                    return [
                        ref[pl.ds(base + shift + TILE * (start + 2 * k), TILE)] for k in range(number)
                    ]

                values = tiles(wide_ref, 0, pairs + 2)
                for k in range(pairs + 1):
                    if shift:
                        add(even, k, weight(0), values[k])
                    add(even, k, weight(16), values[k + 1])
                values = tiles(wide_ref, 1, pairs + 1)
                for k in range(pairs):
                    add(odd, k, weight(8), values[k])
                    add(odd, k, weight(24), values[k + 1])
                values = tiles(sums_ref, 1, pairs + 1)
                for k in range(pairs):
                    add(both, k, weight(32), values[k])
                    add(both, k, weight(40), values[k + 1])
            for k in range(pairs):
                total = jnp.concatenate(
                    [even[k] + odd[k], both[k] - (even[k + 1] + odd[k])], axis=0
                )
                half = 0.5 * total
                place = pl.ds(pl.multiple_of(base + 2 * TILE * k, 2 * TILE), 2 * TILE)
                act_ref[place, out_cols] = (half + half * jnp.tanh(half)).astype(BF16)
            return 0

        lax.fori_loop(0, 2 * frames // STEP, chunk, 0)
        return 0

    lax.fori_loop(0, count, group, 0)


def activation(place, block, other, near, far, taps):
    frames, channels = block.shape
    width = 2 * LANES
    count = channels // width
    rows = 2 * frames + 2 * RIM
    smem, vmem, hbm = (
        pl.BlockSpec(memory_space=space) for space in (pltpu.SMEM, pltpu.VMEM, pltpu.HBM)
    )
    block, taps = (pltpu.with_memory_space_constraint(array, pltpu.HBM) for array in (block, taps))
    return pl.pallas_call(
        conv_kernel,
        in_specs=[smem, hbm, vmem, vmem, vmem, hbm],
        out_specs=vmem,
        out_shape=pltpu.VMEM((2 * frames, channels // 2), BF16),
        scratch_shapes=[
            pltpu.VMEM((count, frames, width), BF16),
            pltpu.VMEM(taps.shape, F32),
            pltpu.VMEM((rows, LANES), F32),
            pltpu.VMEM((rows, LANES), F32),
            pltpu.VMEM((48, LANES), F32),
            pltpu.SemaphoreType.DMA((count + 1,)),
        ],
        compiler_params=PARAMS,
        name="activation",
    )(place, block, other, near, far, taps)


def product_kernel(place_ref, act_ref, own_ref, other_ref, product_ref):
    frames = own_ref.shape[0]
    core = place_ref[0]

    def part(first, signal_ref):
        act = act_ref[pl.ds(pl.multiple_of(first, frames), frames)]
        return lax.dot_general(
            act, signal_ref[...], (((0,), (0,)), ((), ())), preferred_element_type=F32
        )

    total = part(frames * core, own_ref) + part(frames * (1 - core), other_ref)
    blocks, _, quarter, owned, features = product_ref.shape
    pieces = total.reshape(blocks, quarter, 2, owned, features).astype(BF16)
    for parity in range(2):
        product_ref[:, lax.rem(parity + place_ref[1], 2)] = pieces[:, :, parity]


def merge_kernel(inverse_root, parts_ref, carried_ref, right_ref, merged_ref, shares_ref):
    total = parts_ref[0].astype(F32)
    for index in range(1, parts_ref.shape[0]):
        total = total + parts_ref[index].astype(F32)
    merged = total * inverse_root + carried_ref[...]
    merged_ref[...] = merged
    left = lax.dot_general(
        merged, right_ref[...], (((1,), (1,)), ((), ())), precision=HIGHEST, preferred_element_type=F32
    )
    owned = left.shape[0]
    packed = jnp.concatenate([left[: owned // 2], left[owned // 2 :]], axis=1)
    copies = shares_ref.shape[0] * LANES // merged.shape[1]
    for index in range(shares_ref.shape[0]):
        first = LANES * (index // copies)
        shares_ref[index, :owned] = merged[:, first : first + LANES]
        shares_ref[index, owned:] = packed


def term_kernel(place_ref, parts_ref, left_ref, term_ref, rows_ref, gram_ref):
    owned, rank = left_ref.shape
    sources = rows_ref.shape[0]
    lefts, means = [], []
    for source in range(sources):
        total = parts_ref[source]
        for index in range(source + sources, parts_ref.shape[0], sources):
            total = total + parts_ref[index]
        packed = total[owned:]
        left = jnp.concatenate([packed[:, :rank], packed[:, rank:]], axis=0)
        rows_ref[source] = left
        lefts.append(left)
        means.append(total[:owned])
    left_ref[...] = rows_ref[place_ref[3]]
    left, mean = jnp.concatenate(lefts, axis=0), jnp.concatenate(means, axis=0)
    dot = functools.partial(
        lax.dot_general,
        dimension_numbers=(((0,), (0,)), ((), ())),
        precision=HIGHEST,
        preferred_element_type=F32,
    )
    both = dot(left, jnp.concatenate([mean, jnp.zeros_like(left), left], axis=1))
    term = both[:, :LANES]
    gram_ref[...] = both[:, LANES:]
    gram = gram_ref[pl.ds(pl.multiple_of(TILE * place_ref[2], TILE), TILE)]
    gram_ref[...] = term
    term = gram_ref[pl.ds(pl.multiple_of(rank // 2 * place_ref[3], rank // 2), rank // 2)]
    for index in range(term_ref.shape[0]):
        term_ref[index, : rank // 2] = term
        term_ref[index, rank // 2 :] = gram


def join_kernel(halves_ref, total_ref):
    half = halves_ref.shape[1] - TILE
    for index in range(total_ref.shape[0]):
        total_ref[index, :half] = halves_ref[0, :half]
        total_ref[index, half : 2 * half] = halves_ref[1, :half]
        total_ref[index, 2 * half :] = halves_ref[0, half:]


def total_kernel(parts_ref, total_ref):
    total = parts_ref[0]
    for index in range(1, parts_ref.shape[0]):
        total = total + parts_ref[index]
    for index in range(total_ref.shape[0]):
        total_ref[index] = total


def eliminate(rest, rank):
    done = []
    for start in range(0, rank, PANEL):
        row = lax.broadcasted_iota(jnp.int32, rest.shape, 0)
        first = rank + start
        columns = [
            jnp.broadcast_to(rest[:, first + j : first + j + 1], rest.shape) for j in range(PANEL)
        ]
        top = rest[:PANEL]
        scaled = []
        for j in range(PANEL):
            inverse = 1.0 / columns[j][j : j + 1]
            scaled.append(top[j : j + 1] * inverse)
            below = jnp.where(row > j, columns[j], 0.0)
            columns[j] = below
            for i in range(j + 1, PANEL):
                columns[i] = columns[i] - below * (columns[i][j : j + 1] * inverse)
            top = top - below[:PANEL] * scaled[j]
        done.append(top)
        rest = rest[PANEL:]
        if start + PANEL < rank:
            for j in range(PANEL):
                rest = rest - columns[j][PANEL:] * scaled[j]
    return jnp.concatenate(done, axis=0)


def finish_kernel(replicas, rows_ref, left_ref, merged_ref, right_ref, estimate_ref, error_ref, wide_ref):
    rank = left_ref.shape[1]
    features = merged_ref.shape[1]
    for index in range(rows_ref.shape[0]):
        wide_ref[:, LANES * index : LANES * (index + 1)] = rows_ref[index, :rank]
        wide_ref[TILE * index : TILE * (index + 1), features:] = rows_ref[index, rank:]
    row = lax.broadcasted_iota(jnp.int32, (rank, 2 * rank), 0)
    lane = lax.broadcasted_iota(jnp.int32, (rank, 2 * rank), 1)
    work = eliminate(wide_ref[:, features:] + (row == lane).astype(F32), rank)
    pivots = jnp.sum(jnp.where(row + rank == lane, work, 0.0), axis=1, keepdims=True)
    inverse = (work * (1.0 / jnp.sqrt(pivots)))[:, :rank]
    dot = functools.partial(lax.dot_general, precision=HIGHEST, preferred_element_type=F32)
    right = dot(inverse, wide_ref[:, :features], (((1,), (0,)), ((), ()))) * (1.0 / replicas)
    right_ref[...] = right
    left_hat = dot(left_ref[...], inverse, (((1,), (1,)), ((), ())))
    estimate = dot(left_hat, right, (((1,), (0,)), ((), ())))
    estimate_ref[...] = estimate
    error_ref[...] = merged_ref[...] - estimate


def call(kernel, outs, *args, smem=0, scratch=()):
    spaces = [pltpu.SMEM] * smem + [pltpu.VMEM] * (len(args) - smem)
    return pl.pallas_call(
        kernel,
        in_specs=[pl.BlockSpec(memory_space=space) for space in spaces],
        out_shape=[jax.ShapeDtypeStruct(out, F32) if isinstance(out, tuple) else out for out in outs],
        scratch_shapes=list(scratch),
        compiler_params=PARAMS,
        name=getattr(kernel, "func", kernel).__name__,
    )(*args)


def exchange(block, axes, groups=None):
    return lax.all_to_all(block, axes, 0, 0, tiled=True, axis_index_groups=groups)


def local(gated_input, upstream, depth_kernel, carried_error, right_init):
    replicas = lax.axis_size(DP)
    contexts = lax.axis_size(CTX)
    block = gated_input[0]
    frames, channels = block.shape
    features = upstream.shape[2]
    rank = right_init.shape[1]
    owned = channels // contexts
    core = lax.axis_index("c")
    swap = [(0, 1), (1, 0)]
    ends = lax.dynamic_slice_in_dim(block, core * (frames - RIM), RIM, axis=0)
    one = [(i, i + 1 if i % 2 else i - 1) for i in range(1, contexts - 1)]
    two = [(i, i + 2 if i % 2 else i - 2) for i in range(1, contexts - 1)]
    ends, block = lax.optimization_barrier((ends, block))
    near = lax.ppermute(ends, CTX, one)
    far = lax.ppermute(ends, CTX, two)
    other = lax.ppermute(block, "c", swap)
    signal = upstream[0]
    other_signal = lax.ppermute(signal, "c", swap)
    depth = lax.axis_size("z")
    side = [(2 * z) // depth for z in range(depth)]
    teams = [
        [2 * chip + (team + side[chip % depth]) % 2 for chip in range(contexts // 2)]
        for team in range(2)
    ]
    team = lax.rem(core + (2 * lax.axis_index("z")) // depth, 2)
    place = jnp.stack([core, team, lax.axis_index(DP), lax.axis_index("c")])
    act = activation(place, block, other, near, far, depth_kernel)
    (product,) = call(
        product_kernel,
        [pltpu.VMEM((channels // 256, 2, 4, owned, features), BF16)],
        place,
        act,
        signal,
        other_signal,
        smem=1,
    )
    inverse_root = 1.0 / math.sqrt(frames * contexts)
    row = (owned, features)
    spread = lax.axis_size(SPREAD)
    merged, shares = call(
        functools.partial(merge_kernel, inverse_root),
        [row, pltpu.VMEM((spread, owned + owned // 2, LANES), F32)],
        exchange(product.reshape(channels // 32, owned, features), CTX, teams),
        carried_error[0],
        right_init.T,
    )
    size = (rank // 2 + TILE, LANES)
    left, term = call(
        term_kernel,
        [(owned, rank), pltpu.VMEM((lax.axis_size("y"), *size), F32)],
        place,
        exchange(shares, SPREAD),
        smem=1,
        scratch=[pltpu.VMEM((spread // replicas, owned, rank), F32), pltpu.VMEM((rank, LANES), F32)],
    )
    (total,) = call(total_kernel, [pltpu.VMEM((lax.axis_size("z"), *size), F32)], exchange(term, "y"))
    (total,) = call(total_kernel, [(1, *size)], exchange(total, "z"))
    full = pltpu.VMEM((replicas, rank + TILE, LANES), F32)
    (total,) = call(join_kernel, [full], lax.all_gather(total[0], "c"))
    right, estimate, error = call(
        functools.partial(finish_kernel, replicas),
        [(rank, features), row, row],
        exchange(total, DP),
        left,
        merged,
        scratch=[pltpu.VMEM((rank, features + 2 * rank), F32)],
    )
    return right.T, estimate, error[None]


def solution(mesh):
    wide = Mesh(mesh.devices.reshape(4, 2, 4, 8, 2), ("x", "h", "y", "z", "c"))
    return jax.shard_map(
        local,
        mesh=wide,
        in_specs=(P(DP, CTX, None), P(DP, CTX, None), P(), P(DP, CTX, None), P()),
        out_specs=(P(), P(CTX, None), P(DP, CTX, None)),
        check_vma=False,
    )
```
